32 devices in a mesh: blk: 8 (over y, x, core), head: 4 (over z).
Axes of the slice: x: 2, y: 2, z: 4, core: 2. Of those that a mesh axis runs over, the one named last changes fastest.
Arguments:
- queries: bfloat16 [4096, 3072], P(('blk', 'head')), may hold values from -100 to 100
- keys: bfloat16 [4096, 3072], P(('blk', 'head')), may hold values from -100 to 100
- values: bfloat16 [4096, 3072], P(('blk', 'head')), may hold values from -6 to 6
- query_gain: float32 [3072], replicated, may hold values from 1 to 4
- key_gain: float32 [3072], replicated, may hold values from 0.1 to 1.9
Outputs:
- attended: bfloat16 [4096, 3072], P(('blk', 'head'))
The draws below stay inside these ranges and needn't reach their ends.
All inputs are finite; a program needn't handle non-finite values.
Results may differ from the reference program's by a relative error of at most 0.0075.
The reference program's roundings to bfloat16 on the way count: a program that leaves them out, or rounds other values in their place, can miss the bound.
Values may be sent and summed in bfloat16 or wider, within the bound.
No kernel may reach another device: no remote copies, remote signals or barrier semaphores. Data moves between devices by JAX's collectives and lax.ppermute only.
A program may use at most 128 MiB of HBM per device.

```python
import math
import jax
import jax.numpy as jnp
from jax import lax

HEAD_DIM = 128
HEADS = 24
DIM = 3072
TOKENS = 4096


def base_noise(key, salt):
    sub = jax.random.fold_in(key, salt)
    drawn = jnp.clip(jax.random.normal(sub, (TOKENS, DIM), jnp.float32), -6.0, 6.0)
    return drawn


def draw_queries(key, part):
    scaled = base_noise(key, 11)
    return scaled.astype(jnp.bfloat16)


def draw_keys(key, part):
    scaled = base_noise(key, 12)
    return scaled.astype(jnp.bfloat16)


def level_of(stream_key, dims, pieces, low, largest):
    level = 1.0
    for position, shards_of in pieces:
        heights = jax.random.uniform(jax.random.fold_in(jax.random.fold_in(stream_key, 6), position), (shards_of,), jnp.float32, low / len(pieces), largest / len(pieces))
        level = level * jnp.repeat(jnp.exp(heights), dims[position] // shards_of).reshape((-1,) + (1,) * (len(dims) - 1 - position))
    return level


def bell_draw(stream_key, dims, scale, limit, pieces=(), kind=jnp.bfloat16):
    values = scale * jax.random.normal(stream_key, dims, jnp.float32)
    if pieces:
        values = values * level_of(stream_key, dims, pieces, -0.22, 0.18)
    return jnp.clip(values, -limit, limit).astype(kind)


def setup_inputs(seed: int = 0) -> dict:
    key_of = jax.random.split(jax.random.key(seed), 6)
    return {
        "queries": draw_queries(jax.random.fold_in(key_of[5], 71), 0),
        "keys": draw_keys(jax.random.fold_in(key_of[5], 71), 0),
        "values": bell_draw(key_of[2], (TOKENS, DIM), 1.0, 6.0, ((0, 32),)),
        "query_gain": jnp.clip(jnp.exp(jax.random.uniform(key_of[3], (DIM,), jnp.float32, math.log(1.0), math.log(4.0))), 1.0, 4.0),
        "key_gain": jnp.clip(1.0 + 0.18 * jax.random.normal(key_of[4], (DIM,), jnp.float32), 0.1, 1.9),
    }


def normalize(block, gain):
    wide = block.astype(jnp.float32)
    mean_sq = lax.optimization_barrier(jnp.mean(wide * wide, axis=-1, keepdims=True))
    return (wide * lax.rsqrt(mean_sq + 1e-06) * gain).astype(jnp.bfloat16)

def reference(queries, keys, values, query_gain, key_gain):
    normed_q = normalize(queries, query_gain).reshape(TOKENS, HEADS, HEAD_DIM)
    normed_k = normalize(keys, key_gain).reshape(TOKENS, HEADS, HEAD_DIM)
    value_heads = values.reshape(TOKENS, HEADS, HEAD_DIM)
    factor = 1.0 / math.sqrt(HEAD_DIM)
    q_size = math.gcd(TOKENS, 1024)

    def one_head(head_id):
        q_head = lax.dynamic_index_in_dim(normed_q, head_id, 1, keepdims=False)
        k_head = lax.dynamic_index_in_dim(normed_k, head_id, 1, keepdims=False)
        v_head = lax.dynamic_index_in_dim(value_heads, head_id, 1, keepdims=False)

        def one_block(block_id):
            q_rows = lax.dynamic_slice_in_dim(q_head, block_id * q_size, q_size, 0)
            scores = jnp.dot(q_rows, k_head.T, preferred_element_type=jnp.float32) * factor
            top = lax.optimization_barrier(jnp.max(scores, axis=-1, keepdims=True))
            weights = jnp.exp(scores - top)
            total = lax.optimization_barrier(jnp.sum(weights, axis=-1, keepdims=True))
            mixed = jnp.dot(weights.astype(jnp.bfloat16), v_head, preferred_element_type=jnp.float32)
            return (mixed / total).astype(jnp.bfloat16)
        blocks = lax.map(one_block, jnp.arange(TOKENS // q_size).astype(jnp.int32))
        return blocks.reshape(TOKENS, HEAD_DIM)
    result = lax.map(one_head, jnp.arange(HEADS).astype(jnp.int32))
    return jnp.transpose(result, (1, 0, 2)).reshape(TOKENS, DIM)
```

```python
import functools
import math

import jax
import jax.numpy as jnp
from jax import lax
from jax.experimental import pallas as pl
from jax.experimental.pallas import tpu as pltpu
from jax.sharding import PartitionSpec as P

HEAD_DIM = 128
AXES = ("blk", "head")
BF16 = jnp.bfloat16
F32 = jnp.float32
VMEM = pl.BlockSpec(memory_space=pltpu.VMEM)
PARAMS = pltpu.CompilerParams(vmem_limit_bytes=40 * 2**20)
EXPONENT = math.log2(math.e) / math.sqrt(HEAD_DIM)


def sds(*shape):
    return jax.ShapeDtypeStruct(shape, BF16)


def call(body, outs, *args, flops=0, exps=0):
    size = sum(math.prod(a.shape) * a.dtype.itemsize for a in (*args, *outs))
    return pl.pallas_call(
        body,
        out_shape=outs,
        in_specs=[VMEM] * len(args),
        out_specs=[VMEM] * len(outs),
        compiler_params=PARAMS,
        cost_estimate=pl.CostEstimate(flops=flops, bytes_accessed=size, transcendentals=exps),
    )(*args)


def attend_rows(q, keys, values):
    top = total = accum = None
    for k_ref, v_ref in zip(keys, values):
        scores = lax.dot_general(
            q, k_ref[...], (((1,), (1,)), ((), ())), preferred_element_type=F32
        )
        new_top = jnp.max(scores, axis=1, keepdims=True)
        if top is not None:
            new_top = jnp.maximum(top, new_top)
        weights = jnp.exp2((scores - new_top) * EXPONENT)
        part = jnp.sum(weights, axis=1, keepdims=True)
        mixed = jnp.dot(weights.astype(BF16), v_ref[...], preferred_element_type=F32)
        if top is None:
            total, accum = part, mixed
        else:
            shrink = jnp.exp2((top - new_top) * EXPONENT)
            total, accum = total * shrink + part, accum * shrink + mixed
        top = new_top
    return accum / total


def attend_body(slots, blocks, *refs):
    queries, refs = refs[:slots], refs[slots:]
    keys, values, outs = refs[:blocks], refs[blocks : 2 * blocks], refs[2 * blocks :]
    rows = queries[0].shape[0]
    for first in range(0, slots, 2):
        pair = queries[first : first + 2]
        q = jnp.concatenate([ref[...] for ref in pair], axis=0)
        result = attend_rows(q, keys, values).astype(BF16)
        for place in range(len(pair)):
            outs[first + place][...] = result[place * rows : (place + 1) * rows]


def attend(queries, keys, values):
    outs = [sds(*q.shape) for q in queries]
    pairs = sum(q.shape[0] for q in queries) * sum(k.shape[0] for k in keys)
    return call(
        functools.partial(attend_body, len(queries), len(keys)),
        outs,
        *queries,
        *keys,
        *values,
        flops=4 * pairs * HEAD_DIM,
        exps=pairs,
    )


def core_index():
    return lax.rem(lax.axis_index("blk"), 2)


def halves_body(x_ref, other_ref):
    half = x_ref.shape[1] // 2
    other = pl.multiple_of((1 - core_index()) * half, half)
    other_ref[...] = x_ref[:, pl.ds(other, half)]


def normalize_body(x_ref, gain_ref, own_ref, other_ref):
    half = x_ref.shape[1] // 2
    wide = x_ref[...].astype(F32)
    scale = lax.rsqrt(jnp.mean(wide * wide, axis=1, keepdims=True) + 1e-06)
    core = core_index()
    for ref, side in ((own_ref, core), (other_ref, 1 - core)):
        at = pl.ds(pl.multiple_of(side * half, half), half)
        ref[...] = (x_ref[:, at].astype(F32) * scale * gain_ref[:, at]).astype(BF16)


def column(piece, turn):
    z = lax.rem(lax.axis_index("head") + turn, 4)
    return pl.multiple_of(piece * 4 * HEAD_DIM + z * HEAD_DIM, HEAD_DIM)


def pack_body(groups, count, half, *refs):
    ins, outs = refs[:count], refs[count:]
    place = 0
    for pairs in groups:
        for turn in range(4):
            out = outs[place]
            place += 1
            rows = 0
            for tensor, piece in pairs:
                at = column(piece, turn)
                for ref in ins[2 * tensor : 2 * tensor + 2]:
                    tokens = ref.shape[0]
                    start = at
                    if ref.shape[1] != half:
                        start = pl.multiple_of(core_index() * half + at, HEAD_DIM)
                    out[rows : rows + tokens, :] = ref[:, pl.ds(start, HEAD_DIM)]
                    rows += tokens


def pack(groups, tensors):
    flat = [a for pair in tensors for a in pair]
    tokens = flat[0].shape[0]
    outs = [sds(2 * tokens * len(pairs), HEAD_DIM) for pairs in groups for _ in range(4)]
    half = min(a.shape[1] for a in flat)
    made = call(functools.partial(pack_body, groups, len(flat), half), outs, *flat)
    return [made[4 * g : 4 * g + 4] for g in range(len(groups))]


def join_body(parts, *refs):
    ins, outs = refs[:4], refs[4:]
    rows = ins[0].shape[0] // parts
    for part, out in enumerate(outs):
        for turn in range(4):
            out[turn * rows : (turn + 1) * rows, :] = ins[turn][part * rows : (part + 1) * rows, :]


def join(buffers, parts):
    rows = 4 * buffers[0].shape[0] // parts
    return call(functools.partial(join_body, parts), [sds(rows, HEAD_DIM)] * parts, *buffers)


def split_body(*refs):
    ins, out = refs[:-1], refs[-1]
    rows = ins[0].shape[0] // 2
    for turn, ref in enumerate(ins):
        out[turn * rows : (turn + 1) * rows, :] = ref[rows:, :]


def place_body(pieces, *refs):
    out = refs[-1]
    tokens, half = out.shape[0], out.shape[1] // 2
    core = core_index()
    for piece in range(pieces):
        for turn in range(4):
            at = column(piece, turn)
            here = pl.multiple_of(core * half + at, HEAD_DIM)
            there = pl.multiple_of((1 - core) * half + at, HEAD_DIM)
            out[:, pl.ds(here, HEAD_DIM)] = refs[5 * piece + turn][:tokens, :]
            out[:, pl.ds(there, HEAD_DIM)] = refs[5 * piece + 4][
                turn * tokens : (turn + 1) * tokens, :
            ]


def permute(array, move):
    pairs = []
    for y in range(2):
        for x in range(2):
            for core in range(2):
                for z in range(4):
                    to = move(y, x, core, z)
                    pairs.append(
                        ((y * 4 + x * 2 + core) * 4 + z, (to[0] * 4 + to[1] * 2 + to[2]) * 4 + to[3])
                    )
    return lax.ppermute(array, AXES, pairs)


def other_core(array):
    return permute(array, lambda y, x, core, z: (y, x, 1 - core, z))


def other_x(array):
    return permute(array, lambda y, x, core, z: (y, 1 - x, core, z))


def other_y(array):
    return permute(array, lambda y, x, core, z: (1 - y, x, core, z))


def along_z(array, turn):
    return permute(array, lambda y, x, core, z: (y, x, core, (z + turn) % 4))


def rotate(buffers):
    return [buffers[0]] + [along_z(buffers[turn], turn) for turn in (1, 2, 3)]


def rotate_back(buffers):
    return [buffers[0]] + [along_z(buffers[turn], 4 - turn) for turn in (1, 2, 3)]


def gather(keys, values):
    keys_x, values_x = other_x(keys), other_x(values)
    keys_y, values_y = other_y(keys), other_y(values)
    keys_far, values_far = other_x(keys_y), other_y(values_x)
    return (keys, keys_x, keys_y, keys_far), (values, values_x, values_y, values_far)


def shards_fast(queries, keys, values, query_gain, key_gain):
    tokens, width = queries.shape
    half = width // 2
    query_gain, key_gain = query_gain.reshape(1, width), key_gain.reshape(1, width)
    (v_other,) = call(halves_body, [sds(tokens, half)], values)
    v_got = other_core(v_other)
    k_own, k_other = call(normalize_body, [sds(tokens, half)] * 2, keys, key_gain)
    k_got = other_core(k_other)
    q_own, q_other = call(normalize_body, [sds(tokens, half)] * 2, queries, query_gain)
    q_got = other_core(q_other)
    v_pair, k_pair, q_pair = (values, v_got), (k_own, k_got), (q_own, q_got)

    (v0,) = pack([[(0, 0)]], [v_pair])
    v0 = rotate(v0)
    k0, kv1, kv2 = pack([[(0, 0)], [(0, 1), (1, 1)], [(0, 2), (1, 2)]], [k_pair, v_pair])
    k0 = rotate(k0)
    kv1 = rotate(kv1)
    q0, q1, q2 = pack([[(0, 0)], [(0, 1)], [(0, 2)]], [q_pair])
    q0 = rotate(q0)
    kv2 = rotate(kv2)
    q1, q2 = rotate(q1), rotate(q2)

    results = []
    for q_slots, blocks in ((q0, (k0, v0)), (q1, kv1), (q2, kv2)):
        if len(blocks) == 2:
            (key_block,), (value_block,) = join(blocks[0], 1), join(blocks[1], 1)
        else:
            key_block, value_block = join(blocks, 2)
        all_keys, all_values = gather(key_block, value_block)
        back = rotate_back(attend(q_slots, all_keys, all_values))
        (across,) = call(split_body, [sds(4 * tokens, HEAD_DIM)], *back)
        results += [*back, other_core(across)]
    (attended,) = call(functools.partial(place_body, 3), [sds(tokens, width)], *results)
    return attended


def whole_head_body(q_ref, k_ref, v_ref, out_ref, top, total, accum):
    step = pl.program_id(2)

    @pl.when(step == 0)
    def _():
        top[...] = jnp.full_like(top, -jnp.inf)
        total[...] = jnp.zeros_like(total)
        accum[...] = jnp.zeros_like(accum)

    scores = lax.dot_general(
        q_ref[...], k_ref[...], (((1,), (1,)), ((), ())), preferred_element_type=F32
    )
    new_top = jnp.maximum(top[...], jnp.max(scores, axis=1, keepdims=True))
    weights = jnp.exp2((scores - new_top) * EXPONENT)
    shrink = jnp.exp2((top[...] - new_top) * EXPONENT)
    total[...] = total[...] * shrink + jnp.sum(weights, axis=1, keepdims=True)
    accum[...] = accum[...] * shrink + jnp.dot(
        weights.astype(BF16), v_ref[...], preferred_element_type=F32
    )
    top[...] = new_top

    @pl.when(step == pl.num_programs(2) - 1)
    def _():
        out_ref[...] = (accum[...] / total[...]).astype(BF16)


def normalize(block, gain):
    wide = block.astype(F32)
    mean_sq = jnp.mean(wide * wide, axis=-1, keepdims=True)
    return (wide * lax.rsqrt(mean_sq + 1e-06) * gain).astype(BF16)


def shards_any(queries, keys, values, query_gain, key_gain):
    def regroup(x):
        return lax.all_to_all(x, "head", split_axis=1, concat_axis=0, tiled=True)

    q = regroup(normalize(queries, query_gain))
    k = lax.all_gather(regroup(normalize(keys, key_gain)), "blk", axis=0, tiled=True)
    v = lax.all_gather(regroup(values), "blk", axis=0, tiled=True)
    rows, width = q.shape
    length = k.shape[0]
    q_rows, k_rows = math.gcd(rows, 512), math.gcd(length, 1024)
    result = pl.pallas_call(
        whole_head_body,
        grid=(width // HEAD_DIM, rows // q_rows, length // k_rows),
        out_shape=sds(rows, width),
        in_specs=[
            pl.BlockSpec((q_rows, HEAD_DIM), lambda h, i, j: (i, h)),
            pl.BlockSpec((k_rows, HEAD_DIM), lambda h, i, j: (j, h)),
            pl.BlockSpec((k_rows, HEAD_DIM), lambda h, i, j: (j, h)),
        ],
        out_specs=pl.BlockSpec((q_rows, HEAD_DIM), lambda h, i, j: (i, h)),
        scratch_shapes=[
            pltpu.VMEM((q_rows, 1), F32),
            pltpu.VMEM((q_rows, 1), F32),
            pltpu.VMEM((q_rows, HEAD_DIM), F32),
        ],
        compiler_params=PARAMS,
    )(q, k, v)
    return lax.all_to_all(result, "head", split_axis=0, concat_axis=1, tiled=True)


def solution(mesh):
    fast = mesh.shape["blk"] == 8 and mesh.shape["head"] == 4
    rows = P(AXES, None)
    return jax.shard_map(
        shards_fast if fast else shards_any,
        mesh=mesh,
        in_specs=(rows, rows, rows, P(), P()),
        out_specs=rows,
        check_vma=False,
    )
```

```python
import functools
import math

import jax
import jax.numpy as jnp
from jax import lax
from jax.experimental import pallas as pl
from jax.experimental.pallas import tpu as pltpu
from jax.sharding import PartitionSpec as P

HEAD_DIM = 128
AXES = ("blk", "head")
BF16 = jnp.bfloat16
F32 = jnp.float32
VMEM = pl.BlockSpec(memory_space=pltpu.VMEM)
PARAMS = pltpu.CompilerParams(vmem_limit_bytes=40 * 2**20)
EXPONENT = math.log2(math.e) / math.sqrt(HEAD_DIM)


def sds(*shape):
    return jax.ShapeDtypeStruct(shape, BF16)


class Line:
    def __init__(self):
        self.last = ()

    def call(self, body, outs, *args, flops=0, exps=0):
        skip = len(self.last)

        def without_last(*refs):
            body(*refs[skip:])

        size = sum(math.prod(a.shape) * a.dtype.itemsize for a in (*args, *outs))
        made = pl.pallas_call(
            without_last,
            out_shape=outs,
            in_specs=[pl.BlockSpec(memory_space=pl.ANY)] * skip + [VMEM] * len(args),
            out_specs=[VMEM] * len(outs),
            compiler_params=PARAMS,
            cost_estimate=pl.CostEstimate(flops=flops, bytes_accessed=size, transcendentals=exps),
        )(*self.last, *args)
        self.last = made[:1]
        return made


def read(refs, pieces):
    parts = [refs[source][first : first + rows, :] for source, first, rows in pieces]
    return parts[0] if len(parts) == 1 else jnp.concatenate(parts, axis=0)


def absorb(state, q, k, v):
    scores = lax.dot_general(q, k, (((1,), (1,)), ((), ())), preferred_element_type=F32)
    new_top = jnp.max(scores, axis=1, keepdims=True)
    if state is not None:
        top, total, accum = state
        new_top = jnp.maximum(top, new_top)
    weights = jnp.exp2((scores - new_top) * EXPONENT)
    part = jnp.sum(weights, axis=1, keepdims=True)
    mixed = jnp.dot(weights.astype(BF16), v, preferred_element_type=F32)
    if state is not None:
        shrink = jnp.exp2((top - new_top) * EXPONENT)
        part, mixed = total * shrink + part, accum * shrink + mixed
    return new_top, part, mixed


STEP = 512


def attend_body(queries, blocks, count, *refs):
    refs, outs = refs[:count], refs[count:]
    rows = outs[0].shape[0]
    per = STEP // rows
    for first in range(0, len(outs), per):
        q = read(refs, queries[first : first + per])
        state = None
        for keys, values in blocks:
            state = absorb(state, q, read(refs, keys), read(refs, values))
        _, total, accum = state
        result = (accum / total).astype(BF16)
        for place in range(per):
            outs[first + place][...] = result[place * rows : (place + 1) * rows]


class Arrays:
    def __init__(self):
        self.arrays = []

    def piece(self, array, first, rows):
        for place, known in enumerate(self.arrays):
            if known is array:
                return place, first, rows
        self.arrays.append(array)
        return len(self.arrays) - 1, first, rows

    def pieces(self, parts):
        return [self.piece(*part) for part in parts]


def attend(line, queries, blocks):
    known = Arrays()
    queries = known.pieces(queries)
    blocks = [(known.pieces(keys), known.pieces(values)) for keys, values in blocks]
    pairs = sum(q[2] for q in queries) * sum(k[2] for keys, _ in blocks for k in keys)
    return line.call(
        functools.partial(attend_body, queries, blocks, len(known.arrays)),
        [sds(q[2], HEAD_DIM) for q in queries],
        *known.arrays,
        flops=4 * pairs * HEAD_DIM,
        exps=pairs,
    )


def core_index():
    return lax.rem(lax.axis_index("blk"), 2)


def halves_body(x_ref, other_ref):
    half = x_ref.shape[1] // 2
    other = pl.multiple_of((1 - core_index()) * half, half)
    other_ref[...] = x_ref[:, pl.ds(other, half)]


def normalize_body(x_ref, gain_ref, own_ref, other_ref):
    half = x_ref.shape[1] // 2
    wide = x_ref[...].astype(F32)
    scale = lax.rsqrt(jnp.mean(wide * wide, axis=1, keepdims=True) + 1e-06)
    core = core_index()
    for ref, side in ((own_ref, core), (other_ref, 1 - core)):
        at = pl.ds(pl.multiple_of(side * half, half), half)
        ref[...] = (x_ref[:, at].astype(F32) * scale * gain_ref[:, at]).astype(BF16)


def column(piece, hop):
    z = lax.axis_index("head")
    bit, pair = lax.rem(z, 2), lax.div(z, 2)
    bit = 1 - bit if hop & 1 else bit
    pair = 1 - pair if hop & 2 else pair
    return pl.multiple_of((piece * 4 + pair * 2 + bit) * HEAD_DIM, HEAD_DIM)


def pack_body(heads, half, *refs):
    ins, outs = refs[: -len(heads)], refs[-len(heads) :]
    for out, group in zip(outs, heads):
        at = 0
        for tensor, piece, hop in group:
            start = column(piece, hop)
            for ref in ins[2 * tensor : 2 * tensor + 2]:
                tokens = ref.shape[0]
                here = start
                if ref.shape[1] != half:
                    here = pl.multiple_of(core_index() * half + start, HEAD_DIM)
                out[at : at + tokens, :] = ref[:, pl.ds(here, HEAD_DIM)]
                at += tokens


def pack(line, heads, tensors):
    flat = [a for pair in tensors for a in pair]
    tokens = flat[0].shape[0]
    half = min(a.shape[1] for a in flat)
    outs = [sds(2 * tokens * len(group), HEAD_DIM) for group in heads]
    return line.call(functools.partial(pack_body, heads, half), outs, *flat)


def join_body(layout, count, *refs):
    for out, pieces in zip(refs[count:], layout):
        at = 0
        for source, first, rows in pieces:
            out[at : at + rows, :] = refs[source][first : first + rows, :]
            at += rows


def join(line, layout):
    known = Arrays()
    layout = [known.pieces(parts) for parts in layout]
    outs = [sds(sum(rows for _, _, rows in parts), HEAD_DIM) for parts in layout]
    return line.call(functools.partial(join_body, layout, len(known.arrays)), outs, *known.arrays)


def place_body(pieces, *refs):
    out = refs[-1]
    tokens, half = out.shape[0], out.shape[1] // 2
    core = core_index()
    for piece in range(pieces):
        own, across = refs[2 * piece : 2 * piece + 2]
        for hop in range(4):
            at = column(piece, hop)
            here = pl.multiple_of(core * half + at, HEAD_DIM)
            there = pl.multiple_of((1 - core) * half + at, HEAD_DIM)
            rows = slice(hop * tokens, (hop + 1) * tokens)
            out[:, pl.ds(here, HEAD_DIM)] = own[rows, :]
            out[:, pl.ds(there, HEAD_DIM)] = across[rows, :]


def permute(array, move):
    pairs = []
    for y in range(2):
        for x in range(2):
            for core in range(2):
                for z in range(4):
                    to = move(y, x, core, z)
                    pairs.append(
                        ((y * 4 + x * 2 + core) * 4 + z, (to[0] * 4 + to[1] * 2 + to[2]) * 4 + to[3])
                    )
    return lax.ppermute(array, AXES, pairs)


def other_core(array):
    return permute(array, lambda y, x, core, z: (y, x, 1 - core, z))


def other_x(array):
    return permute(array, lambda y, x, core, z: (y, 1 - x, core, z))


def other_y(array):
    return permute(array, lambda y, x, core, z: (1 - y, x, core, z))


def hop_z(array, hop):
    return permute(array, lambda y, x, core, z: (y, x, core, z ^ hop))


def hops(buffers):
    return [hop_z(buffer, hop) for hop, buffer in enumerate(buffers, 1)]


def shards_fast(queries, keys, values, query_gain, key_gain):
    tokens, width = queries.shape
    half, part = width // 2, 2 * tokens
    rest = 3 * part
    query_gain, key_gain = query_gain.reshape(1, width), key_gain.reshape(1, width)
    line = Line()

    def swap_halves(x, gain):
        own, other = line.call(normalize_body, [sds(tokens, half)] * 2, x, gain)
        return own, other_core(other)

    def hand_back(outs):
        back = [outs[0], *hops(outs[1:])]
        layout = [[(a, 0, tokens) for a in back], [(a, tokens, tokens) for a in back]]
        own, across = join(line, layout)
        return own, other_core(across)

    (v_other,) = line.call(halves_body, [sds(tokens, half)], values)
    v_pair = (values, other_core(v_other))
    k_pair = swap_halves(keys, key_gain)
    q_pair = swap_halves(queries, query_gain)
    tensors = (k_pair, v_pair, q_pair)
    k, v, q = range(3)

    out = pack(
        line,
        [[(t, c, 0) for c in range(3) for t in (k, v)]]
        + [[(k, 0, hop), (v, 0, hop)] for hop in (1, 2, 3)],
        tensors[:2],
    )
    own = out[0]
    came = hops(out[1:])
    own_x, own_y = other_x(own), other_y(own)

    def key_rows(array, chunk):
        return array, 2 * chunk * part, part

    def value_rows(array, chunk):
        return array, (2 * chunk + 1) * part, part

    sends, received = [], []
    results = []
    q_slots = []
    for step in range(5):
        if step == 0:
            along_x = [key_rows(own_y, c) for c in range(3)]
            along_y = [value_rows(own_x, c) for c in range(3)]
        elif step < 4:
            got_x, got_y = received[-1]
            along_x = [(got_y, rest, rest)]
            along_y = [(got_x, 2 * rest, rest)]
        if step < 3:
            block = [(a, 0, part) for a in came] + [(a, part, part) for a in came]
            along_x, along_y = along_x + block, along_y + block
        if step < 4:
            x_out, y_out = join(line, [along_x, along_y])
            sends.append(x_out)
            received.append((other_x(x_out), other_y(y_out)))
        if step == 2:
            q_slots.append([(own_q, 0, part)] + [(a, 2 * part, part) for a in came])
        if step == 3:
            for c in (0, 1):
                q_slots.append([(own_q, (c + 1) * part, part)] + [(a, c * part, part) for a in came])
        if step == 0:
            (*out,) = pack(line, [[(k, 1, hop), (v, 1, hop)] for hop in (1, 2, 3)], tensors[:2])
            came = hops(out)
        if step == 1:
            own_q, *out = pack(
                line,
                [[(q, c, 0) for c in range(3)]]
                + [[(k, 2, hop), (v, 2, hop), (q, 0, hop)] for hop in (1, 2, 3)],
                tensors,
            )
            came = hops(out)
        if step == 2:
            out = pack(line, [[(0, 1, hop), (0, 2, hop)] for hop in (1, 2, 3)], (q_pair,))
            came = hops(out)
        if step >= 2:
            chunk = step - 2
            got_x, got_y = received[chunk]
            far_x, far_y = received[chunk + 1]
            blocks = []
            for mine, more in ((own, sends[chunk]), (own_x, got_x), (own_y, got_y)):
                blocks.append(
                    (
                        [key_rows(mine, chunk), (more, rest, rest)],
                        [value_rows(mine, chunk), (more, 2 * rest, rest)],
                    )
                )
            first_x, first_y = received[0]
            blocks.append(
                (
                    [(first_x, chunk * part, part), (far_x, 0, rest)],
                    [(first_y, chunk * part, part), (far_y, 0, rest)],
                )
            )
            results += hand_back(attend(line, q_slots[chunk], blocks))
    (attended,) = line.call(functools.partial(place_body, 3), [sds(tokens, width)], *results)
    return attended


def whole_head_body(q_ref, k_ref, v_ref, out_ref, top, total, accum):
    step = pl.program_id(2)

    @pl.when(step == 0)
    def _():
        top[...] = jnp.full_like(top, -jnp.inf)
        total[...] = jnp.zeros_like(total)
        accum[...] = jnp.zeros_like(accum)

    scores = lax.dot_general(
        q_ref[...], k_ref[...], (((1,), (1,)), ((), ())), preferred_element_type=F32
    )
    new_top = jnp.maximum(top[...], jnp.max(scores, axis=1, keepdims=True))
    weights = jnp.exp2((scores - new_top) * EXPONENT)
    shrink = jnp.exp2((top[...] - new_top) * EXPONENT)
    total[...] = total[...] * shrink + jnp.sum(weights, axis=1, keepdims=True)
    accum[...] = accum[...] * shrink + jnp.dot(
        weights.astype(BF16), v_ref[...], preferred_element_type=F32
    )
    top[...] = new_top

    @pl.when(step == pl.num_programs(2) - 1)
    def _():
        out_ref[...] = (accum[...] / total[...]).astype(BF16)


def normalize(block, gain):
    wide = block.astype(F32)
    mean_sq = jnp.mean(wide * wide, axis=-1, keepdims=True)
    return (wide * lax.rsqrt(mean_sq + 1e-06) * gain).astype(BF16)


def shards_any(queries, keys, values, query_gain, key_gain):
    def regroup(x):
        return lax.all_to_all(x, "head", split_axis=1, concat_axis=0, tiled=True)

    q = regroup(normalize(queries, query_gain))
    k = lax.all_gather(regroup(normalize(keys, key_gain)), "blk", axis=0, tiled=True)
    v = lax.all_gather(regroup(values), "blk", axis=0, tiled=True)
    rows, width = q.shape
    length = k.shape[0]
    q_rows, k_rows = math.gcd(rows, 512), math.gcd(length, 1024)
    result = pl.pallas_call(
        whole_head_body,
        grid=(width // HEAD_DIM, rows // q_rows, length // k_rows),
        out_shape=sds(rows, width),
        in_specs=[
            pl.BlockSpec((q_rows, HEAD_DIM), lambda h, i, j: (i, h)),
            pl.BlockSpec((k_rows, HEAD_DIM), lambda h, i, j: (j, h)),
            pl.BlockSpec((k_rows, HEAD_DIM), lambda h, i, j: (j, h)),
        ],
        out_specs=pl.BlockSpec((q_rows, HEAD_DIM), lambda h, i, j: (i, h)),
        scratch_shapes=[
            pltpu.VMEM((q_rows, 1), F32),
            pltpu.VMEM((q_rows, 1), F32),
            pltpu.VMEM((q_rows, HEAD_DIM), F32),
        ],
        compiler_params=PARAMS,
    )(q, k, v)
    return lax.all_to_all(result, "head", split_axis=0, concat_axis=1, tiled=True)


def solution(mesh):
    fast = mesh.shape["blk"] == 8 and mesh.shape["head"] == 4
    rows = P(AXES, None)
    return jax.shard_map(
        shards_fast if fast else shards_any,
        mesh=mesh,
        in_specs=(rows, rows, rows, P(), P()),
        out_specs=rows,
        check_vma=False,
    )
```

```python
import functools
import math

import jax
import jax.numpy as jnp
from jax import lax
from jax.experimental import pallas as pl
from jax.experimental.pallas import tpu as pltpu
from jax.sharding import PartitionSpec as P

HEAD_DIM = 128
AXES = ("blk", "head")
BF16 = jnp.bfloat16
F32 = jnp.float32
VMEM = pl.BlockSpec(memory_space=pltpu.VMEM)
PARAMS = pltpu.CompilerParams(vmem_limit_bytes=40 * 2**20)
EXPONENT = math.log2(math.e) / math.sqrt(HEAD_DIM)


def sds(*shape):
    return jax.ShapeDtypeStruct(shape, BF16)


class Line:
    def __init__(self):
        self.last = ()

    def call(self, body, outs, *args, after=(), flops=0, exps=0):
        behind = (*self.last, *after)
        skip = len(behind)

        def without_last(*refs):
            body(*refs[skip:])

        size = sum(math.prod(a.shape) * a.dtype.itemsize for a in (*args, *outs))
        made = pl.pallas_call(
            without_last,
            out_shape=outs,
            in_specs=[pl.BlockSpec(memory_space=pl.ANY)] * skip + [VMEM] * len(args),
            out_specs=[VMEM] * len(outs),
            compiler_params=PARAMS,
            cost_estimate=pl.CostEstimate(flops=flops, bytes_accessed=size, transcendentals=exps),
        )(*behind, *args)
        self.last = made[:1]
        return made


def read(refs, pieces):
    parts = [refs[source][first : first + rows, :] for source, first, rows in pieces]
    return parts[0] if len(parts) == 1 else jnp.concatenate(parts, axis=0)


def absorb(state, q, k, v):
    scores = lax.dot_general(q, k, (((1,), (1,)), ((), ())), preferred_element_type=F32)
    new_top = jnp.max(scores, axis=1, keepdims=True)
    if state is not None:
        top, total, accum = state
        new_top = jnp.maximum(top, new_top)
    weights = jnp.exp2((scores - new_top) * EXPONENT)
    part = jnp.sum(weights, axis=1, keepdims=True)
    mixed = jnp.dot(weights.astype(BF16), v, preferred_element_type=F32)
    if state is not None:
        shrink = jnp.exp2((top - new_top) * EXPONENT)
        part, mixed = total * shrink + part, accum * shrink + mixed
    return new_top, part, mixed


def attend_body(queries, blocks, count, *refs):
    refs, outs = refs[:count], refs[count:]
    for pair in range(0, len(queries), 2):
        q = read(refs, queries[pair : pair + 2])
        state = None
        for keys, values in blocks:
            state = absorb(state, q, read(refs, keys), read(refs, values))
        _, total, accum = state
        result = (accum / total).astype(BF16)
        first = pair // 2 * q.shape[0]
        at = 0
        for out in outs:
            low, high = max(at, first), min(at + out.shape[0], first + q.shape[0])
            if low < high:
                out[low - at : high - at, :] = result[low - first : high - first, :]
            at += out.shape[0]


class Arrays:
    def __init__(self):
        self.arrays = []

    def piece(self, array, first, rows):
        for place, known in enumerate(self.arrays):
            if known is array:
                return place, first, rows
        self.arrays.append(array)
        return len(self.arrays) - 1, first, rows

    def pieces(self, parts):
        return [self.piece(*part) for part in parts]


def attend(line, queries, blocks, outs):
    known = Arrays()
    queries = known.pieces(queries)
    blocks = [(known.pieces(keys), known.pieces(values)) for keys, values in blocks]
    pairs = sum(outs) * sum(k[2] for keys, _ in blocks for k in keys)
    return line.call(
        functools.partial(attend_body, queries, blocks, len(known.arrays)),
        [sds(rows, HEAD_DIM) for rows in outs],
        *known.arrays,
        flops=4 * pairs * HEAD_DIM,
        exps=pairs,
    )


KEPT, SECOND, FIRST, OPPOSITE = range(4)
HOPS = (KEPT, SECOND, FIRST, OPPOSITE)


def core_index():
    return lax.rem(lax.axis_index("blk"), 2)


def halves_body(x_ref, other_ref):
    half = x_ref.shape[1] // 2
    other = pl.multiple_of((1 - core_index()) * half, half)
    other_ref[...] = x_ref[:, pl.ds(other, half)]


def normalize_body(x_ref, gain_ref, own_ref, other_ref):
    half = x_ref.shape[1] // 2
    wide = x_ref[...].astype(F32)
    scale = lax.rsqrt(jnp.mean(wide * wide, axis=1, keepdims=True) + 1e-06)
    core = core_index()
    for ref, side in ((own_ref, core), (other_ref, 1 - core)):
        at = pl.ds(pl.multiple_of(side * half, half), half)
        ref[...] = (x_ref[:, at].astype(F32) * scale * gain_ref[:, at]).astype(BF16)


def column(piece, hop):
    z, core = lax.axis_index("head"), core_index()
    low, high = lax.rem(z, 2), lax.div(z, 2)
    if hop in (FIRST, OPPOSITE):
        low, high = lax.rem(low + core, 2), lax.rem(high + 1 - core, 2)
    if hop in (SECOND, OPPOSITE):
        low, high = lax.rem(low + 1 - core, 2), lax.rem(high + core, 2)
    return pl.multiple_of((piece * 4 + high * 2 + low) * HEAD_DIM, HEAD_DIM)


def pack_body(heads, half, *refs):
    ins, outs = refs[: -len(heads)], refs[-len(heads) :]
    for out, group in zip(outs, heads):
        at = 0
        for tensor, piece, hop in group:
            start = column(piece, hop)
            for ref in ins[2 * tensor : 2 * tensor + 2]:
                tokens = ref.shape[0]
                here = start
                if ref.shape[1] != half:
                    here = pl.multiple_of(core_index() * half + start, HEAD_DIM)
                out[at : at + tokens, :] = ref[:, pl.ds(here, HEAD_DIM)]
                at += tokens


def pack(line, heads, tensors, after=()):
    flat = [a for pair in tensors for a in pair]
    tokens = flat[0].shape[0]
    half = min(a.shape[1] for a in flat)
    outs = [sds(2 * tokens * len(group), HEAD_DIM) for group in heads]
    return line.call(functools.partial(pack_body, heads, half), outs, *flat, after=after)


def join_body(layout, count, *refs):
    for out, pieces in zip(refs[count:], layout):
        at = 0
        for source, first, rows in pieces:
            out[at : at + rows, :] = refs[source][first : first + rows, :]
            at += rows


def join(line, layout, after=()):
    known = Arrays()
    layout = [known.pieces(parts) for parts in layout]
    outs = [sds(sum(rows for _, _, rows in parts), HEAD_DIM) for parts in layout]
    return line.call(
        functools.partial(join_body, layout, len(known.arrays)), outs, *known.arrays, after=after
    )


def place_body(pieces, *refs):
    out = refs[-1]
    tokens, half = out.shape[0], out.shape[1] // 2
    core = core_index()
    for piece in range(pieces):
        own, across = refs[2 * piece : 2 * piece + 2]
        for hop in HOPS:
            at = column(piece, hop)
            here = pl.multiple_of(core * half + at, HEAD_DIM)
            there = pl.multiple_of((1 - core) * half + at, HEAD_DIM)
            rows = slice(hop * tokens, (hop + 1) * tokens)
            out[:, pl.ds(here, HEAD_DIM)] = own[rows, :]
            out[:, pl.ds(there, HEAD_DIM)] = across[rows, :]


def permute(array, move):
    pairs = []
    for y in range(2):
        for x in range(2):
            for core in range(2):
                for z in range(4):
                    to = move(y, x, core, z)
                    pairs.append(
                        ((y * 4 + x * 2 + core) * 4 + z, (to[0] * 4 + to[1] * 2 + to[2]) * 4 + to[3])
                    )
    return lax.ppermute(array, AXES, pairs)


def other_core(array):
    return permute(array, lambda y, x, core, z: (y, x, 1 - core, z))


def hop_z(array, hop):
    def move(y, x, core, z):
        first, second = (2, 1) if core == 0 else (1, 2)
        return y, x, core, z ^ {FIRST: first, SECOND: second, OPPOSITE: 3}[hop]

    return permute(array, move)


def hop_xy(array, hop):
    def move(y, x, core, z):
        return (y, 1 - x, core, z) if (hop == FIRST) == (core == 0) else (1 - y, x, core, z)

    return permute(array, move)


def shards_fast(queries, keys, values, query_gain, key_gain):
    tokens, width = queries.shape
    half, part = width // 2, 2 * tokens
    rest = 3 * part
    query_gain, key_gain = query_gain.reshape(1, width), key_gain.reshape(1, width)
    line = Line()

    def swap_halves(x, gain):
        own, other = line.call(normalize_body, [sds(tokens, half)] * 2, x, gain)
        return own, other_core(other)

    (v_other,) = line.call(halves_body, [sds(tokens, half)], values)
    v_pair = (values, other_core(v_other))
    k_pair = swap_halves(keys, key_gain)
    q_pair = swap_halves(queries, query_gain)
    tensors = (k_pair, v_pair, q_pair)
    k, v, q = range(3)

    def swap(heads, after=()):
        used = sorted({t for t, _ in heads})
        groups = [[(used.index(t), c, hop) for t, c in heads] for hop in HOPS[1:]]
        outs = pack(line, groups, [tensors[t] for t in used], after)
        return [hop_z(out, hop) for hop, out in zip(HOPS[1:], outs)]

    def slots(swapped, first, rows):
        return [(array, first, rows) for array in swapped]

    def send_xy(far, swapped):
        block = slots(swapped, 0, part) + slots(swapped, part, part)
        whole = [(far, 0, far.shape[0])]
        out, both = join(line, [block, whole + block])
        got = hop_xy(both, FIRST)
        return out, got, hop_xy(out, SECOND)

    def blocks_of(chunk, sent, far):
        block, got, got_second = sent
        four = (
            (own, 0, block, 0),
            (own_first, 0, got, got.shape[0] - 2 * rest),
            (own_second, 0, got_second, 0),
            (sent0[1], 0, far, 0),
        )
        blocks = []
        for kept, kept_at, array, at in four:
            kept_at += 2 * chunk * part
            keys = [(kept, kept_at, part), (array, at, rest)]
            blocks.append((keys, [(a, first + rows, rows) for a, first, rows in keys]))
        return [
            (low[0] + high[0], low[1] + high[1]) for low, high in zip(blocks[::2], blocks[1::2])
        ]

    def queries_of(chunk, swapped, first):
        return dict(zip(HOPS, [(own_q, chunk * part, part)] + slots(swapped, first, part)))

    def core_swap(back):
        kept, second, first, opposite = back
        other = kept, first, second, opposite
        layout = [[(a, 0, tokens) for a in back], [(a, tokens, tokens) for a in other]]
        own, across = join(line, layout)
        return own, other_core(across)

    def attend_back(slots, blocks, hops):
        outs = attend(line, [slots[hop] for hop in hops], blocks, [part] * len(hops))
        return {hop: out if hop == KEPT else hop_z(out, hop) for hop, out in zip(hops, outs)}

    def by_hop(back):
        return [back[hop] for hop in HOPS]

    group0, group1 = [(k, 0), (v, 0)], [(k, 1), (v, 1)]
    group2, group3 = [(k, 2), (v, 2), (q, 0)], [(q, 1), (q, 2)]

    swap0 = swap(group0)
    (own,) = pack(line, [[(t, c, KEPT) for c in range(3) for t in (k, v)]], tensors[:2])
    own_first, own_second = hop_xy(own, FIRST), hop_xy(own, SECOND)
    swap1 = swap(group1, after=(*swap0, own_first, own_second))
    sent0 = send_xy(own_second, swap0)
    swap2 = swap(group2, after=(*swap1, *sent0))
    sent1 = send_xy(sent0[2], swap1)
    swap3 = swap(group3, after=(*swap2, *sent1))
    sent2 = send_xy(sent1[2], swap2)
    (own_q,) = pack(line, [[(0, c, KEPT) for c in range(3)]], (q_pair,))
    back0 = attend_back(
        queries_of(0, swap2, 2 * part), blocks_of(0, sent0, sent1[1]), (OPPOSITE, FIRST, KEPT, SECOND)
    )
    (last,) = join(line, [[(sent2[2], 0, 2 * rest)]], after=swap3)
    far = hop_xy(last, FIRST)
    back1 = attend_back(
        queries_of(1, swap3, 0), blocks_of(1, sent1, sent2[1]), (OPPOSITE, FIRST, KEPT, SECOND)
    )
    results = core_swap(by_hop(back0))
    slots2, blocks2 = queries_of(2, swap3, part), blocks_of(2, sent2, far)
    back2 = attend_back(slots2, blocks2, (OPPOSITE, FIRST, KEPT, SECOND))
    results += core_swap(by_hop(back1))
    results += core_swap(by_hop(back2))
    (attended,) = line.call(functools.partial(place_body, 3), [sds(tokens, width)], *results)
    return attended


def whole_head_body(q_ref, k_ref, v_ref, out_ref, top, total, accum):
    step = pl.program_id(2)

    @pl.when(step == 0)
    def _():
        top[...] = jnp.full_like(top, -jnp.inf)
        total[...] = jnp.zeros_like(total)
        accum[...] = jnp.zeros_like(accum)

    scores = lax.dot_general(
        q_ref[...], k_ref[...], (((1,), (1,)), ((), ())), preferred_element_type=F32
    )
    new_top = jnp.maximum(top[...], jnp.max(scores, axis=1, keepdims=True))
    weights = jnp.exp2((scores - new_top) * EXPONENT)
    shrink = jnp.exp2((top[...] - new_top) * EXPONENT)
    total[...] = total[...] * shrink + jnp.sum(weights, axis=1, keepdims=True)
    accum[...] = accum[...] * shrink + jnp.dot(
        weights.astype(BF16), v_ref[...], preferred_element_type=F32
    )
    top[...] = new_top

    @pl.when(step == pl.num_programs(2) - 1)
    def _():
        out_ref[...] = (accum[...] / total[...]).astype(BF16)


def normalize(block, gain):
    wide = block.astype(F32)
    mean_sq = jnp.mean(wide * wide, axis=-1, keepdims=True)
    return (wide * lax.rsqrt(mean_sq + 1e-06) * gain).astype(BF16)


def shards_any(queries, keys, values, query_gain, key_gain):
    def regroup(x):
        return lax.all_to_all(x, "head", split_axis=1, concat_axis=0, tiled=True)

    q = regroup(normalize(queries, query_gain))
    k = lax.all_gather(regroup(normalize(keys, key_gain)), "blk", axis=0, tiled=True)
    v = lax.all_gather(regroup(values), "blk", axis=0, tiled=True)
    rows, width = q.shape
    length = k.shape[0]
    q_rows, k_rows = math.gcd(rows, 512), math.gcd(length, 1024)
    result = pl.pallas_call(
        whole_head_body,
        grid=(width // HEAD_DIM, rows // q_rows, length // k_rows),
        out_shape=sds(rows, width),
        in_specs=[
            pl.BlockSpec((q_rows, HEAD_DIM), lambda h, i, j: (i, h)),
            pl.BlockSpec((k_rows, HEAD_DIM), lambda h, i, j: (j, h)),
            pl.BlockSpec((k_rows, HEAD_DIM), lambda h, i, j: (j, h)),
        ],
        out_specs=pl.BlockSpec((q_rows, HEAD_DIM), lambda h, i, j: (i, h)),
        scratch_shapes=[
            pltpu.VMEM((q_rows, 1), F32),
            pltpu.VMEM((q_rows, 1), F32),
            pltpu.VMEM((q_rows, HEAD_DIM), F32),
        ],
        compiler_params=PARAMS,
    )(q, k, v)
    return lax.all_to_all(result, "head", split_axis=0, concat_axis=1, tiled=True)


def solution(mesh):
    fast = mesh.shape["blk"] == 8 and mesh.shape["head"] == 4
    rows = P(AXES, None)
    return jax.shard_map(
        shards_fast if fast else shards_any,
        mesh=mesh,
        in_specs=(rows, rows, rows, P(), P()),
        out_specs=rows,
        check_vma=False,
    )
```

```python
import functools
import math

import jax
import jax.numpy as jnp
from jax import lax
from jax.experimental import pallas as pl
from jax.experimental.pallas import tpu as pltpu
from jax.sharding import PartitionSpec as P

HEAD_DIM = 128
AXES = ("blk", "head")
BF16 = jnp.bfloat16
F32 = jnp.float32
VMEM = pl.BlockSpec(memory_space=pltpu.VMEM)
PARAMS = pltpu.CompilerParams(vmem_limit_bytes=40 * 2**20)
EXPONENT = math.log2(math.e) / math.sqrt(HEAD_DIM)


def nothing_body(out):
    out[...] = jnp.zeros_like(out)


def sds(*shape):
    return jax.ShapeDtypeStruct(shape, BF16)


class Line:
    def __init__(self):
        self.last = ()

    def call(self, body, outs, *args, after=(), flops=0, exps=0):
        behind = (*self.last, *after)
        skip = len(behind)

        def without_last(*refs):
            body(*refs[skip:])

        size = sum(math.prod(a.shape) * a.dtype.itemsize for a in (*args, *outs))
        made = pl.pallas_call(
            without_last,
            out_shape=outs,
            in_specs=[pl.BlockSpec(memory_space=pl.ANY)] * skip
            + [VMEM] * len(args),
            out_specs=[VMEM] * len(outs),
            compiler_params=PARAMS,
            cost_estimate=pl.CostEstimate(flops=flops, bytes_accessed=size, transcendentals=exps),
        )(*behind, *args)
        self.last = made[:1]
        return made

    def mark(self):
        self.call(nothing_body, [sds(16, HEAD_DIM)], flops=2 * 10**10)


def read(refs, pieces):
    parts = [refs[source][first : first + rows, :] for source, first, rows in pieces]
    return parts[0] if len(parts) == 1 else jnp.concatenate(parts, axis=0)


def absorb(state, q, k, v):
    scores = lax.dot_general(q, k, (((1,), (1,)), ((), ())), preferred_element_type=F32)
    new_top = jnp.max(scores, axis=1, keepdims=True)
    if state is not None:
        top, total, accum = state
        new_top = jnp.maximum(top, new_top)
    weights = jnp.exp2((scores - new_top) * EXPONENT)
    part = jnp.sum(weights, axis=1, keepdims=True)
    mixed = jnp.dot(weights.astype(BF16), v, preferred_element_type=F32)
    if state is not None:
        shrink = jnp.exp2((top - new_top) * EXPONENT)
        part, mixed = total * shrink + part, accum * shrink + mixed
    return new_top, part, mixed


def attend_body(queries, blocks, count, *refs):
    refs, outs = refs[:count], refs[count:]
    for pair in range(0, len(queries), 2):
        q = read(refs, queries[pair : pair + 2])
        state = None
        for keys, values in blocks:
            state = absorb(state, q, read(refs, keys), read(refs, values))
        _, total, accum = state
        result = (accum / total).astype(BF16)
        first = pair // 2 * q.shape[0]
        at = 0
        for out in outs:
            low, high = max(at, first), min(at + out.shape[0], first + q.shape[0])
            if low < high:
                out[low - at : high - at, :] = result[low - first : high - first, :]
            at += out.shape[0]


class Arrays:
    def __init__(self):
        self.arrays = []

    def piece(self, array, first, rows):
        for place, known in enumerate(self.arrays):
            if known is array:
                return place, first, rows
        self.arrays.append(array)
        return len(self.arrays) - 1, first, rows

    def pieces(self, parts):
        return [self.piece(*part) for part in parts]


def attend(line, queries, blocks, outs):
    known = Arrays()
    queries = known.pieces(queries)
    blocks = [(known.pieces(keys), known.pieces(values)) for keys, values in blocks]
    pairs = sum(outs) * sum(k[2] for keys, _ in blocks for k in keys)
    return line.call(
        functools.partial(attend_body, queries, blocks, len(known.arrays)),
        [sds(rows, HEAD_DIM) for rows in outs],
        *known.arrays,
        flops=4 * pairs * HEAD_DIM,
        exps=pairs,
    )


KEPT, SECOND, FIRST, OPPOSITE = range(4)
HOPS = (KEPT, SECOND, FIRST, OPPOSITE)


def core_index():
    return lax.rem(lax.axis_index("blk"), 2)


def halves_body(x_ref, other_ref):
    half = x_ref.shape[1] // 2
    other = pl.multiple_of((1 - core_index()) * half, half)
    other_ref[...] = x_ref[:, pl.ds(other, half)]


def normalize_body(x_ref, gain_ref, own_ref, other_ref):
    half = x_ref.shape[1] // 2
    wide = x_ref[...].astype(F32)
    scale = lax.rsqrt(jnp.mean(wide * wide, axis=1, keepdims=True) + 1e-06)
    core = core_index()
    for ref, side in ((own_ref, core), (other_ref, 1 - core)):
        at = pl.ds(pl.multiple_of(side * half, half), half)
        ref[...] = (x_ref[:, at].astype(F32) * scale * gain_ref[:, at]).astype(BF16)


def column(piece, hop):
    z, core = lax.axis_index("head"), core_index()
    low, high = lax.rem(z, 2), lax.div(z, 2)
    if hop in (FIRST, OPPOSITE):
        low, high = lax.rem(low + core, 2), lax.rem(high + 1 - core, 2)
    if hop in (SECOND, OPPOSITE):
        low, high = lax.rem(low + 1 - core, 2), lax.rem(high + core, 2)
    return pl.multiple_of((piece * 4 + high * 2 + low) * HEAD_DIM, HEAD_DIM)


def pack_body(heads, half, *refs):
    ins, outs = refs[: -len(heads)], refs[-len(heads) :]
    for out, group in zip(outs, heads):
        at = 0
        for tensor, piece, hop in group:
            start = column(piece, hop)
            for ref in ins[2 * tensor : 2 * tensor + 2]:
                tokens = ref.shape[0]
                here = start
                if ref.shape[1] != half:
                    here = pl.multiple_of(core_index() * half + start, HEAD_DIM)
                out[at : at + tokens, :] = ref[:, pl.ds(here, HEAD_DIM)]
                at += tokens


def pack(line, heads, tensors, after=()):
    flat = [a for pair in tensors for a in pair]
    tokens = flat[0].shape[0]
    half = min(a.shape[1] for a in flat)
    outs = [sds(2 * tokens * len(group), HEAD_DIM) for group in heads]
    return line.call(functools.partial(pack_body, heads, half), outs, *flat, after=after)


def join_body(layout, count, *refs):
    for out, pieces in zip(refs[count:], layout):
        at = 0
        for source, first, rows in pieces:
            out[at : at + rows, :] = refs[source][first : first + rows, :]
            at += rows


def join(line, layout, after=()):
    known = Arrays()
    layout = [known.pieces(parts) for parts in layout]
    outs = [sds(sum(rows for _, _, rows in parts), HEAD_DIM) for parts in layout]
    return line.call(
        functools.partial(join_body, layout, len(known.arrays)), outs, *known.arrays, after=after
    )


def place_body(own, across, out):
    tokens, half = out.shape[0], out.shape[1] // 2
    core = core_index()
    for at in range(0, own.shape[0], tokens):
        place = column(at // tokens // 4, at // tokens % 4)
        here = pl.multiple_of(core * half + place, HEAD_DIM)
        there = pl.multiple_of((1 - core) * half + place, HEAD_DIM)
        rows = slice(at, at + tokens)
        out[:, pl.ds(here, HEAD_DIM)] = own[rows, :]
        out[:, pl.ds(there, HEAD_DIM)] = across[rows, :]


def permute(array, move):
    pairs = []
    for y in range(2):
        for x in range(2):
            for core in range(2):
                for z in range(4):
                    to = move(y, x, core, z)
                    pairs.append(
                        ((y * 4 + x * 2 + core) * 4 + z, (to[0] * 4 + to[1] * 2 + to[2]) * 4 + to[3])
                    )
    return lax.ppermute(array, AXES, pairs)


def other_core(array):
    return permute(array, lambda y, x, core, z: (y, x, 1 - core, z))


def hop_z(array, hop):
    def move(y, x, core, z):
        first, second = (2, 1) if core == 0 else (1, 2)
        return y, x, core, z ^ {FIRST: first, SECOND: second, OPPOSITE: 3}[hop]

    return permute(array, move)


def hop_xy(array, hop):
    def move(y, x, core, z):
        return (y, 1 - x, core, z) if (hop == FIRST) == (core == 0) else (1 - y, x, core, z)

    return permute(array, move)


def shards_fast(queries, keys, values, query_gain, key_gain):
    tokens, width = queries.shape
    half, part = width // 2, 2 * tokens
    rest = 3 * part
    query_gain, key_gain = query_gain.reshape(1, width), key_gain.reshape(1, width)
    line = Line()

    def swap_halves(x, gain):
        own, other = line.call(normalize_body, [sds(tokens, half)] * 2, x, gain)
        return own, other_core(other)

    k_pair = swap_halves(keys, key_gain)
    (v_other,) = line.call(halves_body, [sds(tokens, half)], values)
    v_pair = (values, other_core(v_other))
    q_pair = swap_halves(queries, query_gain)
    tensors = (k_pair, v_pair, q_pair)
    k, v, q = range(3)

    def swap(heads, after=()):
        used = sorted({t for t, _ in heads})
        groups = [[(used.index(t), c, hop) for t, c in heads] for hop in HOPS[1:]]
        outs = pack(line, groups, [tensors[t] for t in used], after)
        return [hop_z(out, hop) for hop, out in zip(HOPS[1:], outs)]

    def slots(swapped, first, rows):
        return [(array, first, rows) for array in swapped]

    def start_gather(swapped):
        (block,) = join(line, [slots(swapped, 0, part) + slots(swapped, part, part)])
        return block, hop_xy(block, FIRST)

    def end_gather(block, got, after=()):
        rows = block.shape[0]
        (both,) = join(line, [[(block, 0, rows), (got, 0, rows)]], after)
        more = hop_xy(both, SECOND)
        return [(block, 0), (got, 0), (more, 0), (more, rows)]

    def blocks_of(chunk, gathered):
        blocks = []
        for (kept, kept_at), (array, at) in zip(own_gathered, gathered):
            keys = [(kept, kept_at + 2 * chunk * part, part), (array, at, rest)]
            blocks.append((keys, [(a, first + rows, rows) for a, first, rows in keys]))
        return [
            (low[0] + high[0], low[1] + high[1]) for low, high in zip(blocks[::2], blocks[1::2])
        ]

    def queries_of(chunk, swapped, first):
        return dict(zip(HOPS, [(own_q, chunk * part, part)] + slots(swapped, first, part)))

    def core_swap(groups):
        own, other = [], []
        for back, chunks in groups:
            kept, second, first, opposite = back
            for c in range(chunks):
                own += [(a, 2 * c * tokens, tokens) for a in back]
                other += [(a, (2 * c + 1) * tokens, tokens) for a in (kept, first, second, opposite)]
        own, across = join(line, [own, other])
        return own, other_core(across)

    def send_back(outs):
        return [outs[KEPT]] + [hop_z(outs[hop], hop) for hop in HOPS[1:]]

    group0, group1 = [(k, 0), (v, 0)], [(k, 1), (v, 1)]
    group2, group3 = [(k, 2), (v, 2), (q, 0)], [(q, 1), (q, 2)]
    outs = [part] * 4

    swap0 = swap(group0)
    (own,) = pack(line, [[(t, c, KEPT) for c in range(3) for t in (k, v)]], tensors[:2])
    own_got = hop_xy(own, FIRST)
    line.mark()
    swap1 = swap(group1, after=(*swap0, own_got))
    own_gathered = end_gather(own, own_got)
    gather0 = start_gather(swap0)
    line.mark()
    swap2 = swap(group2, after=(*swap1, own_gathered[2][0], gather0[1]))
    gathered0 = end_gather(*gather0)
    gather1 = start_gather(swap1)
    line.mark()
    swap3 = swap(group3, after=(*swap2, gathered0[2][0], gather1[1]))
    gathered1 = end_gather(*gather1)
    gather2 = start_gather(swap2)
    (own_q,) = pack(line, [[(0, c, KEPT) for c in range(3)]], (q_pair,))
    out0 = attend(line, list(queries_of(0, swap2, 2 * part).values()), blocks_of(0, gathered0), outs)
    gathered2 = end_gather(*gather2, after=swap3)
    out1 = attend(line, list(queries_of(1, swap3, 0).values()), blocks_of(1, gathered1), outs)
    back01 = send_back(join(line, [[(x, 0, part), (y, 0, part)] for x, y in zip(out0, out1)]))
    out2 = attend(line, list(queries_of(2, swap3, part).values()), blocks_of(2, gathered2), outs)
    results = core_swap([(back01, 2), (send_back(out2), 1)])
    (attended,) = line.call(place_body, [sds(tokens, width)], *results)
    return attended


def whole_head_body(q_ref, k_ref, v_ref, out_ref, top, total, accum):
    step = pl.program_id(2)

    @pl.when(step == 0)
    def _():
        top[...] = jnp.full_like(top, -jnp.inf)
        total[...] = jnp.zeros_like(total)
        accum[...] = jnp.zeros_like(accum)

    scores = lax.dot_general(
        q_ref[...], k_ref[...], (((1,), (1,)), ((), ())), preferred_element_type=F32
    )
    new_top = jnp.maximum(top[...], jnp.max(scores, axis=1, keepdims=True))
    weights = jnp.exp2((scores - new_top) * EXPONENT)
    shrink = jnp.exp2((top[...] - new_top) * EXPONENT)
    total[...] = total[...] * shrink + jnp.sum(weights, axis=1, keepdims=True)
    accum[...] = accum[...] * shrink + jnp.dot(
        weights.astype(BF16), v_ref[...], preferred_element_type=F32
    )
    top[...] = new_top

    @pl.when(step == pl.num_programs(2) - 1)
    def _():
        out_ref[...] = (accum[...] / total[...]).astype(BF16)


def normalize(block, gain):
    wide = block.astype(F32)
    mean_sq = jnp.mean(wide * wide, axis=-1, keepdims=True)
    return (wide * lax.rsqrt(mean_sq + 1e-06) * gain).astype(BF16)


def shards_any(queries, keys, values, query_gain, key_gain):
    def regroup(x):
        return lax.all_to_all(x, "head", split_axis=1, concat_axis=0, tiled=True)

    q = regroup(normalize(queries, query_gain))
    k = lax.all_gather(regroup(normalize(keys, key_gain)), "blk", axis=0, tiled=True)
    v = lax.all_gather(regroup(values), "blk", axis=0, tiled=True)
    rows, width = q.shape
    length = k.shape[0]
    q_rows, k_rows = math.gcd(rows, 512), math.gcd(length, 1024)
    result = pl.pallas_call(
        whole_head_body,
        grid=(width // HEAD_DIM, rows // q_rows, length // k_rows),
        out_shape=sds(rows, width),
        in_specs=[
            pl.BlockSpec((q_rows, HEAD_DIM), lambda h, i, j: (i, h)),
            pl.BlockSpec((k_rows, HEAD_DIM), lambda h, i, j: (j, h)),
            pl.BlockSpec((k_rows, HEAD_DIM), lambda h, i, j: (j, h)),
        ],
        out_specs=pl.BlockSpec((q_rows, HEAD_DIM), lambda h, i, j: (i, h)),
        scratch_shapes=[
            pltpu.VMEM((q_rows, 1), F32),
            pltpu.VMEM((q_rows, 1), F32),
            pltpu.VMEM((q_rows, HEAD_DIM), F32),
        ],
        compiler_params=PARAMS,
    )(q, k, v)
    return lax.all_to_all(result, "head", split_axis=0, concat_axis=1, tiled=True)


def solution(mesh):
    fast = mesh.shape["blk"] == 8 and mesh.shape["head"] == 4
    rows = P(AXES, None)
    return jax.shard_map(
        shards_fast if fast else shards_any,
        mesh=mesh,
        in_specs=(rows, rows, rows, P(), P()),
        out_specs=rows,
        check_vma=False,
    )
```

```python
import functools
import math

import jax
import jax.numpy as jnp
from jax import lax
from jax.experimental import pallas as pl
from jax.experimental.pallas import tpu as pltpu
from jax.sharding import PartitionSpec as P

HEAD_DIM = 128
AXES = ("blk", "head")
BF16 = jnp.bfloat16
F32 = jnp.float32
VMEM = pl.BlockSpec(memory_space=pltpu.VMEM)
PARAMS = pltpu.CompilerParams(vmem_limit_bytes=40 * 2**20)
EXPONENT = math.log2(math.e) / math.sqrt(HEAD_DIM)


def nothing_body(out):
    out[...] = jnp.zeros_like(out)


def sds(*shape):
    return jax.ShapeDtypeStruct(shape, BF16)


class Line:
    def __init__(self):
        self.last = ()

    def call(self, body, outs, *args, after=(), flops=0, exps=0):
        behind = (*self.last, *after)
        skip = len(behind)

        def without_last(*refs):
            body(*refs[skip:])

        size = sum(math.prod(a.shape) * a.dtype.itemsize for a in (*args, *outs))
        made = pl.pallas_call(
            without_last,
            out_shape=outs,
            in_specs=[pl.BlockSpec(memory_space=pl.ANY)] * skip
            + [VMEM] * len(args),
            out_specs=[VMEM] * len(outs),
            compiler_params=PARAMS,
            cost_estimate=pl.CostEstimate(flops=flops, bytes_accessed=size, transcendentals=exps),
        )(*behind, *args)
        self.last = made[:1]
        return made

    def mark(self):
        self.call(nothing_body, [sds(16, HEAD_DIM)], flops=2 * 10**10)


def read(refs, pieces):
    parts = [refs[source][first : first + rows, :] for source, first, rows in pieces]
    return parts[0] if len(parts) == 1 else jnp.concatenate(parts, axis=0)


def absorb(state, q, k, v):
    scores = lax.dot_general(q, k, (((1,), (1,)), ((), ())), preferred_element_type=F32)
    new_top = jnp.max(scores, axis=1, keepdims=True)
    if state is not None:
        top, total, accum = state
        new_top = jnp.maximum(top, new_top)
    weights = jnp.exp2((scores - new_top) * EXPONENT)
    part = jnp.sum(weights, axis=1, keepdims=True)
    mixed = jnp.dot(weights.astype(BF16), v, preferred_element_type=F32)
    if state is not None:
        shrink = jnp.exp2((top - new_top) * EXPONENT)
        part, mixed = total * shrink + part, accum * shrink + mixed
    return new_top, part, mixed


def attend_body(queries, blocks, count, *refs):
    refs, outs = refs[:count], refs[count:]
    for pair in range(0, len(queries), 2):
        q = read(refs, queries[pair : pair + 2])
        state = None
        for keys, values in blocks:
            state = absorb(state, q, read(refs, keys), read(refs, values))
        _, total, accum = state
        result = (accum / total).astype(BF16)
        first = pair // 2 * q.shape[0]
        at = 0
        for out in outs:
            low, high = max(at, first), min(at + out.shape[0], first + q.shape[0])
            if low < high:
                out[low - at : high - at, :] = result[low - first : high - first, :]
            at += out.shape[0]


class Arrays:
    def __init__(self):
        self.arrays = []

    def piece(self, array, first, rows):
        for place, known in enumerate(self.arrays):
            if known is array:
                return place, first, rows
        self.arrays.append(array)
        return len(self.arrays) - 1, first, rows

    def pieces(self, parts):
        return [self.piece(*part) for part in parts]


def attend(line, queries, blocks, outs):
    known = Arrays()
    queries = known.pieces(queries)
    blocks = [(known.pieces(keys), known.pieces(values)) for keys, values in blocks]
    pairs = sum(outs) * sum(k[2] for keys, _ in blocks for k in keys)
    return line.call(
        functools.partial(attend_body, queries, blocks, len(known.arrays)),
        [sds(rows, HEAD_DIM) for rows in outs],
        *known.arrays,
        flops=4 * pairs * HEAD_DIM,
        exps=pairs,
    )


KEPT, SECOND, FIRST, OPPOSITE = range(4)
HOPS = (KEPT, SECOND, FIRST, OPPOSITE)


def core_index():
    return lax.rem(lax.axis_index("blk"), 2)


def halves_body(x_ref, other_ref):
    half = x_ref.shape[1] // 2
    other = pl.multiple_of((1 - core_index()) * half, half)
    other_ref[...] = x_ref[:, pl.ds(other, half)]


def normalize_body(x_ref, gain_ref, own_ref, other_ref):
    half = x_ref.shape[1] // 2
    wide = x_ref[...].astype(F32)
    scale = lax.rsqrt(jnp.mean(wide * wide, axis=1, keepdims=True) + 1e-06)
    core = core_index()
    for ref, side in ((own_ref, core), (other_ref, 1 - core)):
        at = pl.ds(pl.multiple_of(side * half, half), half)
        ref[...] = (x_ref[:, at].astype(F32) * scale * gain_ref[:, at]).astype(BF16)


def column(piece, hop):
    z, core = lax.axis_index("head"), core_index()
    low, high = lax.rem(z, 2), lax.div(z, 2)
    if hop in (FIRST, OPPOSITE):
        low, high = lax.rem(low + core, 2), lax.rem(high + 1 - core, 2)
    if hop in (SECOND, OPPOSITE):
        low, high = lax.rem(low + 1 - core, 2), lax.rem(high + core, 2)
    return pl.multiple_of((piece * 4 + high * 2 + low) * HEAD_DIM, HEAD_DIM)


def pack_body(heads, half, *refs):
    ins, outs = refs[: -len(heads)], refs[-len(heads) :]
    for out, group in zip(outs, heads):
        at = 0
        for tensor, piece, hop in group:
            start = column(piece, hop)
            for ref in ins[2 * tensor : 2 * tensor + 2]:
                tokens = ref.shape[0]
                here = start
                if ref.shape[1] != half:
                    here = pl.multiple_of(core_index() * half + start, HEAD_DIM)
                out[at : at + tokens, :] = ref[:, pl.ds(here, HEAD_DIM)]
                at += tokens


def pack(line, heads, tensors, after=()):
    flat = [a for pair in tensors for a in pair]
    tokens = flat[0].shape[0]
    half = min(a.shape[1] for a in flat)
    outs = [sds(2 * tokens * len(group), HEAD_DIM) for group in heads]
    return line.call(functools.partial(pack_body, heads, half), outs, *flat, after=after)


def join_body(layout, count, *refs):
    for out, pieces in zip(refs[count:], layout):
        at = 0
        for source, first, rows in pieces:
            out[at : at + rows, :] = refs[source][first : first + rows, :]
            at += rows


def join(line, layout, after=()):
    known = Arrays()
    layout = [known.pieces(parts) for parts in layout]
    outs = [sds(sum(rows for _, _, rows in parts), HEAD_DIM) for parts in layout]
    return line.call(
        functools.partial(join_body, layout, len(known.arrays)), outs, *known.arrays, after=after
    )


def place_body(*refs):
    out = refs[-1]
    tokens, half = out.shape[0], out.shape[1] // 2
    core = core_index()
    place = 0
    for own, across in zip(refs[:-1:2], refs[1:-1:2]):
        for at in range(0, own.shape[0], tokens):
            start = column(place // 4, place % 4)
            here = pl.multiple_of(core * half + start, HEAD_DIM)
            there = pl.multiple_of((1 - core) * half + start, HEAD_DIM)
            rows = slice(at, at + tokens)
            out[:, pl.ds(here, HEAD_DIM)] = own[rows, :]
            out[:, pl.ds(there, HEAD_DIM)] = across[rows, :]
            place += 1


def permute(array, move):
    pairs = []
    for y in range(2):
        for x in range(2):
            for core in range(2):
                for z in range(4):
                    to = move(y, x, core, z)
                    pairs.append(
                        ((y * 4 + x * 2 + core) * 4 + z, (to[0] * 4 + to[1] * 2 + to[2]) * 4 + to[3])
                    )
    return lax.ppermute(array, AXES, pairs)


def other_core(array):
    return permute(array, lambda y, x, core, z: (y, x, 1 - core, z))


def hop_z(array, hop):
    def move(y, x, core, z):
        first, second = (2, 1) if core == 0 else (1, 2)
        return y, x, core, z ^ {FIRST: first, SECOND: second, OPPOSITE: 3}[hop]

    return permute(array, move)


def hop_xy(array, hop):
    def move(y, x, core, z):
        return (y, 1 - x, core, z) if (hop == FIRST) == (core == 0) else (1 - y, x, core, z)

    return permute(array, move)


def shards_fast(queries, keys, values, query_gain, key_gain):
    tokens, width = queries.shape
    half, part = width // 2, 2 * tokens
    rest = 3 * part
    query_gain, key_gain = query_gain.reshape(1, width), key_gain.reshape(1, width)
    line = Line()

    def swap_halves(x, gain):
        own, other = line.call(normalize_body, [sds(tokens, half)] * 2, x, gain)
        return own, other_core(other)

    k_pair = swap_halves(keys, key_gain)
    (v_other,) = line.call(halves_body, [sds(tokens, half)], values)
    v_pair = (values, other_core(v_other))
    q_pair = swap_halves(queries, query_gain)
    tensors = (k_pair, v_pair, q_pair)
    k, v, q = range(3)

    def swap(heads, after=()):
        used = sorted({t for t, _ in heads})
        groups = [[(used.index(t), c, hop) for t, c in heads] for hop in HOPS[1:]]
        outs = pack(line, groups, [tensors[t] for t in used], after)
        return [hop_z(out, hop) for hop, out in zip(HOPS[1:], outs)]

    def slots(swapped, first, rows):
        return [(array, first, rows) for array in swapped]

    def start_gather(swapped, *ahead):
        layout = slots(swapped, 0, part) + slots(swapped, part, part)
        (block,) = join(line, [[(a, 0, a.shape[0]) for a in ahead] + layout])
        return block, hop_xy(block, FIRST)

    def end_gather(block, got, skip=0, after=()):
        rows = block.shape[0] - skip
        (both,) = join(line, [[(block, skip, rows), (got, skip, rows)]], after)
        more = hop_xy(both, SECOND)
        return [(block, skip), (got, skip), (more, 0), (more, rows)]

    def blocks_of(chunk, gathered):
        blocks = []
        for (kept, kept_at), (array, at) in zip(own_gathered, gathered):
            keys = [(kept, kept_at + 2 * chunk * part, part), (array, at, rest)]
            blocks.append((keys, [(a, first + rows, rows) for a, first, rows in keys]))
        return [
            (low[0] + high[0], low[1] + high[1]) for low, high in zip(blocks[::2], blocks[1::2])
        ]

    def queries_of(chunk, swapped, first):
        return dict(zip(HOPS, [(own_q, chunk * part, part)] + slots(swapped, first, part)))

    def core_swap(back, chunks):
        kept, second, first, opposite = back
        own, other = [], []
        for c in range(chunks):
            own += [(a, 2 * c * tokens, tokens) for a in back]
            other += [(a, (2 * c + 1) * tokens, tokens) for a in (kept, first, second, opposite)]
        own, across = join(line, [own, other])
        return own, other_core(across)

    def send_back(outs):
        return [outs[KEPT]] + [hop_z(outs[hop], hop) for hop in HOPS[1:]]

    group0, group1 = [(k, 0), (v, 0)], [(k, 1), (v, 1)]
    group2, group3 = [(k, 2), (v, 2), (q, 0)], [(q, 1), (q, 2)]
    outs = [part] * 4

    swap0 = swap(group0)
    (own,) = pack(line, [[(t, c, KEPT) for c in range(3) for t in (k, v)]], tensors[:2])
    own_first, own_second = hop_xy(own, FIRST), hop_xy(own, SECOND)
    line.mark()
    swap1 = swap(group1, after=(*swap0, own_first, own_second))
    gather0 = start_gather(swap0, own_second)
    line.mark()
    swap2 = swap(group2, after=(*swap1, gather0[1]))
    skip = own.shape[0]
    own_gathered = [(own, 0), (own_first, 0), (own_second, 0), (gather0[1], 0)]
    gathered0 = end_gather(*gather0, skip)
    gather1 = start_gather(swap1)
    line.mark()
    swap3 = swap(group3, after=(*swap2, gathered0[2][0], gather1[1]))
    gathered1 = end_gather(*gather1)
    gather2 = start_gather(swap2)
    (own_q,) = pack(line, [[(0, c, KEPT) for c in range(3)]], (q_pair,))
    out0 = attend(line, list(queries_of(0, swap2, 2 * part).values()), blocks_of(0, gathered0), outs)
    gathered2 = end_gather(*gather2, after=swap3)
    out1 = attend(line, list(queries_of(1, swap3, 0).values()), blocks_of(1, gathered1), outs)
    back01 = send_back(join(line, [[(x, 0, part), (y, 0, part)] for x, y in zip(out0, out1)]))
    out2 = attend(line, list(queries_of(2, swap3, part).values()), blocks_of(2, gathered2), outs)
    back2 = send_back(out2)
    results = core_swap(back01, 2)
    line.mark()
    results += core_swap(back2, 1)
    (attended,) = line.call(place_body, [sds(tokens, width)], *results)
    return attended


def whole_head_body(q_ref, k_ref, v_ref, out_ref, top, total, accum):
    step = pl.program_id(2)

    @pl.when(step == 0)
    def _():
        top[...] = jnp.full_like(top, -jnp.inf)
        total[...] = jnp.zeros_like(total)
        accum[...] = jnp.zeros_like(accum)

    scores = lax.dot_general(
        q_ref[...], k_ref[...], (((1,), (1,)), ((), ())), preferred_element_type=F32
    )
    new_top = jnp.maximum(top[...], jnp.max(scores, axis=1, keepdims=True))
    weights = jnp.exp2((scores - new_top) * EXPONENT)
    shrink = jnp.exp2((top[...] - new_top) * EXPONENT)
    total[...] = total[...] * shrink + jnp.sum(weights, axis=1, keepdims=True)
    accum[...] = accum[...] * shrink + jnp.dot(
        weights.astype(BF16), v_ref[...], preferred_element_type=F32
    )
    top[...] = new_top

    @pl.when(step == pl.num_programs(2) - 1)
    def _():
        out_ref[...] = (accum[...] / total[...]).astype(BF16)


def normalize(block, gain):
    wide = block.astype(F32)
    mean_sq = jnp.mean(wide * wide, axis=-1, keepdims=True)
    return (wide * lax.rsqrt(mean_sq + 1e-06) * gain).astype(BF16)


def shards_any(queries, keys, values, query_gain, key_gain):
    def regroup(x):
        return lax.all_to_all(x, "head", split_axis=1, concat_axis=0, tiled=True)

    q = regroup(normalize(queries, query_gain))
    k = lax.all_gather(regroup(normalize(keys, key_gain)), "blk", axis=0, tiled=True)
    v = lax.all_gather(regroup(values), "blk", axis=0, tiled=True)
    rows, width = q.shape
    length = k.shape[0]
    q_rows, k_rows = math.gcd(rows, 512), math.gcd(length, 1024)
    result = pl.pallas_call(
        whole_head_body,
        grid=(width // HEAD_DIM, rows // q_rows, length // k_rows),
        out_shape=sds(rows, width),
        in_specs=[
            pl.BlockSpec((q_rows, HEAD_DIM), lambda h, i, j: (i, h)),
            pl.BlockSpec((k_rows, HEAD_DIM), lambda h, i, j: (j, h)),
            pl.BlockSpec((k_rows, HEAD_DIM), lambda h, i, j: (j, h)),
        ],
        out_specs=pl.BlockSpec((q_rows, HEAD_DIM), lambda h, i, j: (i, h)),
        scratch_shapes=[
            pltpu.VMEM((q_rows, 1), F32),
            pltpu.VMEM((q_rows, 1), F32),
            pltpu.VMEM((q_rows, HEAD_DIM), F32),
        ],
        compiler_params=PARAMS,
    )(q, k, v)
    return lax.all_to_all(result, "head", split_axis=0, concat_axis=1, tiled=True)


def solution(mesh):
    fast = mesh.shape["blk"] == 8 and mesh.shape["head"] == 4
    rows = P(AXES, None)
    return jax.shard_map(
        shards_fast if fast else shards_any,
        mesh=mesh,
        in_specs=(rows, rows, rows, P(), P()),
        out_specs=rows,
        check_vma=False,
    )
```

```python
import functools
import math

import jax
import jax.numpy as jnp
from jax import lax
from jax.experimental import pallas as pl
from jax.experimental.pallas import tpu as pltpu
from jax.sharding import PartitionSpec as P

HEAD_DIM = 128
AXES = ("blk", "head")
BF16 = jnp.bfloat16
F32 = jnp.float32
VMEM = pl.BlockSpec(memory_space=pltpu.VMEM)
PARAMS = pltpu.CompilerParams(vmem_limit_bytes=40 * 2**20)
EXPONENT = math.log2(math.e) / math.sqrt(HEAD_DIM)


def nothing_body(out):
    out[...] = jnp.zeros_like(out)


def sds(*shape):
    return jax.ShapeDtypeStruct(shape, BF16)


class Line:
    def __init__(self):
        self.last = ()

    def call(self, body, outs, *args, after=(), flops=0, exps=0):
        behind = (*self.last, *after)
        skip = len(behind)

        def without_last(*refs):
            body(*refs[skip:])

        size = sum(math.prod(a.shape) * a.dtype.itemsize for a in (*args, *outs))
        made = pl.pallas_call(
            without_last,
            out_shape=outs,
            in_specs=[pl.BlockSpec(memory_space=pl.ANY)] * skip
            + [VMEM] * len(args),
            out_specs=[VMEM] * len(outs),
            compiler_params=PARAMS,
            cost_estimate=pl.CostEstimate(flops=flops, bytes_accessed=size, transcendentals=exps),
        )(*behind, *args)
        self.last = made[:1]
        return made

    def place(self, body, outs, *args, onto=None):
        behind = self.last if onto is None else (onto,)
        tokens = outs[0].shape[0]

        def without_last(*refs):
            body(*refs[len(behind) :])

        made = pl.pallas_call(
            without_last,
            out_shape=outs,
            in_specs=[pl.BlockSpec(memory_space=pl.ANY)] * len(behind) + [VMEM] * len(args),
            out_specs=[pl.BlockSpec(memory_space=pl.ANY)],
            scratch_shapes=[
                pltpu.SemaphoreType.DMA((sum(a.shape[0] for a in args) // tokens,))
            ],
            input_output_aliases={} if onto is None else {0: 0},
            compiler_params=PARAMS,
        )(*behind, *args)
        self.last = made[:1]
        return made

    def mark(self):
        self.call(nothing_body, [sds(16, HEAD_DIM)], flops=2 * 10**10)


def read(refs, pieces):
    parts = [refs[source][first : first + rows, :] for source, first, rows in pieces]
    return parts[0] if len(parts) == 1 else jnp.concatenate(parts, axis=0)


def scores_of(q, k):
    return lax.dot_general(q, k, (((1,), (1,)), ((), ())), preferred_element_type=F32)


def absorb(state, scores, v):
    new_top = jnp.max(scores, axis=1, keepdims=True)
    if state is not None:
        top, accum = state
        new_top = jnp.maximum(top, new_top)
    weights = jnp.exp2((scores - new_top) * EXPONENT)
    both = jnp.concatenate([v, jnp.ones_like(v)], axis=1)
    mixed = jnp.dot(weights.astype(BF16), both, preferred_element_type=F32)
    if state is not None:
        mixed = accum * jnp.exp2((top - new_top) * EXPONENT) + mixed
    return new_top, mixed


def attend_body(queries, blocks, count, *refs):
    refs, outs = refs[:count], refs[count:]
    steps = [(pair, block) for pair in range(0, len(queries), 2) for block in blocks]

    def scores_at(step):
        pair, (keys, _) = steps[step]
        return scores_of(read(refs, queries[pair : pair + 2]), read(refs, keys))

    ahead = scores_at(0)
    state = None
    for step, (pair, (keys, values)) in enumerate(steps):
        scores = ahead
        if step + 1 < len(steps):
            ahead = scores_at(step + 1)
        if keys is blocks[0][0]:
            state = None
        state = absorb(state, scores, read(refs, values))
        if keys is not blocks[-1][0]:
            continue
        accum = state[1]
        result = (accum[:, :HEAD_DIM] / accum[:, HEAD_DIM:]).astype(BF16)
        first = pair // 2 * result.shape[0]
        at = 0
        for out in outs:
            low, high = max(at, first), min(at + out.shape[0], first + result.shape[0])
            if low < high:
                out[low - at : high - at, :] = result[low - first : high - first, :]
            at += out.shape[0]


class Arrays:
    def __init__(self):
        self.arrays = []

    def piece(self, array, first, rows):
        for place, known in enumerate(self.arrays):
            if known is array:
                return place, first, rows
        self.arrays.append(array)
        return len(self.arrays) - 1, first, rows

    def pieces(self, parts):
        return [self.piece(*part) for part in parts]


def attend(line, queries, blocks, outs):
    known = Arrays()
    queries = known.pieces(queries)
    blocks = [(known.pieces(keys), known.pieces(values)) for keys, values in blocks]
    pairs = sum(outs) * sum(k[2] for keys, _ in blocks for k in keys)
    return line.call(
        functools.partial(attend_body, queries, blocks, len(known.arrays)),
        [sds(rows, HEAD_DIM) for rows in outs],
        *known.arrays,
        flops=4 * pairs * HEAD_DIM,
        exps=pairs,
    )


KEPT, SECOND, FIRST, OPPOSITE = range(4)
HOPS = (KEPT, SECOND, FIRST, OPPOSITE)


def core_index():
    return lax.rem(lax.axis_index("blk"), 2)


def halves_body(x_ref, other_ref):
    half = x_ref.shape[1] // 2
    other = pl.multiple_of((1 - core_index()) * half, half)
    other_ref[...] = x_ref[:, pl.ds(other, half)]


def normalize_body(x_ref, gain_ref, own_ref, other_ref):
    half = x_ref.shape[1] // 2
    wide = x_ref[...].astype(F32)
    scale = lax.rsqrt(jnp.mean(wide * wide, axis=1, keepdims=True) + 1e-06)
    core = core_index()
    for ref, side in ((own_ref, core), (other_ref, 1 - core)):
        at = pl.ds(pl.multiple_of(side * half, half), half)
        ref[...] = (x_ref[:, at].astype(F32) * scale * gain_ref[:, at]).astype(BF16)


def column(piece, hop):
    z, core = lax.axis_index("head"), core_index()
    low, high = lax.rem(z, 2), lax.div(z, 2)
    if hop in (FIRST, OPPOSITE):
        low, high = lax.rem(low + core, 2), lax.rem(high + 1 - core, 2)
    if hop in (SECOND, OPPOSITE):
        low, high = lax.rem(low + 1 - core, 2), lax.rem(high + core, 2)
    return pl.multiple_of((piece * 4 + high * 2 + low) * HEAD_DIM, HEAD_DIM)


def pack_body(heads, half, *refs):
    ins, outs = refs[: -len(heads)], refs[-len(heads) :]
    for out, group in zip(outs, heads):
        at = 0
        for tensor, piece, hop in group:
            start = column(piece, hop)
            for ref in ins[2 * tensor : 2 * tensor + 2]:
                tokens = ref.shape[0]
                here = start
                if ref.shape[1] != half:
                    here = pl.multiple_of(core_index() * half + start, HEAD_DIM)
                out[at : at + tokens, :] = ref[:, pl.ds(here, HEAD_DIM)]
                at += tokens


def pack(line, heads, tensors, after=()):
    flat = [a for pair in tensors for a in pair]
    tokens = flat[0].shape[0]
    half = min(a.shape[1] for a in flat)
    outs = [sds(2 * tokens * len(group), HEAD_DIM) for group in heads]
    return line.call(functools.partial(pack_body, heads, half), outs, *flat, after=after)


def join_body(layout, count, *refs):
    for out, pieces in zip(refs[count:], layout):
        at = 0
        for source, first, rows in pieces:
            out[at : at + rows, :] = refs[source][first : first + rows, :]
            at += rows


def join(line, layout, after=()):
    known = Arrays()
    layout = [known.pieces(parts) for parts in layout]
    outs = [sds(sum(rows for _, _, rows in parts), HEAD_DIM) for parts in layout]
    return line.call(
        functools.partial(join_body, layout, len(known.arrays)), outs, *known.arrays, after=after
    )


def place_body(parts, *refs):
    out, sems = refs[-2:]
    tokens, half = out.shape[0], out.shape[1] // 2
    copies = []
    for ref, (chunk, across) in zip(refs, parts):
        core = 1 - core_index() if across else core_index()
        for place in range(ref.shape[0] // tokens):
            start = core * half + column(chunk + place // 4, place % 4)
            columns = pl.ds(pl.multiple_of(start, HEAD_DIM), HEAD_DIM)
            rows = pl.ds(place * tokens, tokens)
            copies.append(
                pltpu.make_async_copy(ref.at[rows], out.at[:, columns], sems.at[len(copies)])
            )
    for copy in copies:
        copy.start()
    for copy in copies:
        copy.wait()


def permute(array, move):
    pairs = []
    for y in range(2):
        for x in range(2):
            for core in range(2):
                for z in range(4):
                    to = move(y, x, core, z)
                    pairs.append(
                        ((y * 4 + x * 2 + core) * 4 + z, (to[0] * 4 + to[1] * 2 + to[2]) * 4 + to[3])
                    )
    return lax.ppermute(array, AXES, pairs)


def other_core(array):
    return permute(array, lambda y, x, core, z: (y, x, 1 - core, z))


def hop_z(array, hop):
    def move(y, x, core, z):
        first, second = (2, 1) if core == 0 else (1, 2)
        return y, x, core, z ^ {FIRST: first, SECOND: second, OPPOSITE: 3}[hop]

    return permute(array, move)


def hop_xy(array, hop):
    def move(y, x, core, z):
        return (y, 1 - x, core, z) if (hop == FIRST) == (core == 0) else (1 - y, x, core, z)

    return permute(array, move)


def shards_fast(queries, keys, values, query_gain, key_gain):
    tokens, width = queries.shape
    half, part = width // 2, 2 * tokens
    rest = 3 * part
    query_gain, key_gain = query_gain.reshape(1, width), key_gain.reshape(1, width)
    line = Line()

    def swap_halves(x, gain):
        own, other = line.call(normalize_body, [sds(tokens, half)] * 2, x, gain)
        return own, other_core(other)

    k_pair = swap_halves(keys, key_gain)
    (v_other,) = line.call(halves_body, [sds(tokens, half)], values)
    v_pair = (values, other_core(v_other))
    q_pair = swap_halves(queries, query_gain)
    tensors = (k_pair, v_pair, q_pair)
    k, v, q = range(3)

    def swap(heads, after=()):
        used = sorted({t for t, _ in heads})
        groups = [[(used.index(t), c, hop) for t, c in heads] for hop in HOPS[1:]]
        outs = pack(line, groups, [tensors[t] for t in used], after)
        return [hop_z(out, hop) for hop, out in zip(HOPS[1:], outs)]

    def slots(swapped, first, rows):
        return [(array, first, rows) for array in swapped]

    def start_gather(swapped, *ahead):
        layout = slots(swapped, 0, part) + slots(swapped, part, part)
        (block,) = join(line, [[(a, 0, a.shape[0]) for a in ahead] + layout])
        return block, hop_xy(block, FIRST)

    def end_gather(block, got, skip=0, after=()):
        rows = block.shape[0] - skip
        (both,) = join(line, [[(block, skip, rows), (got, skip, rows)]], after)
        more = hop_xy(both, SECOND)
        return [(block, skip), (got, skip), (more, 0), (more, rows)]

    def blocks_of(chunk, gathered):
        blocks = []
        for (kept, kept_at), (array, at) in zip(own_gathered, gathered):
            keys = [(kept, kept_at + 2 * chunk * part, part), (array, at, rest)]
            blocks.append((keys, [(a, first + rows, rows) for a, first, rows in keys]))
        return [
            (low[0] + high[0], low[1] + high[1]) for low, high in zip(blocks[::2], blocks[1::2])
        ]

    def queries_of(chunk, swapped, first):
        return dict(zip(HOPS, [(own_q, chunk * part, part)] + slots(swapped, first, part)))

    def core_swap(back, chunks):
        kept, second, first, opposite = back
        own, other = [], []
        for c in range(chunks):
            own += [(a, 2 * c * tokens, tokens) for a in back]
            other += [(a, (2 * c + 1) * tokens, tokens) for a in (kept, first, second, opposite)]
        own, across = join(line, [own, other])
        return own, other_core(across)

    def send_back(outs):
        return [outs[KEPT]] + [hop_z(outs[hop], hop) for hop in HOPS[1:]]

    group0, group1 = [(k, 0), (v, 0)], [(k, 1), (v, 1)]
    group2, group3 = [(k, 2), (v, 2), (q, 0)], [(q, 1), (q, 2)]
    outs = [part] * 4

    swap0 = swap(group0)
    (own,) = pack(line, [[(t, c, KEPT) for c in range(3) for t in (k, v)]], tensors[:2])
    own_first, own_second = hop_xy(own, FIRST), hop_xy(own, SECOND)
    line.mark()
    swap1 = swap(group1, after=(*swap0, own_first, own_second))
    gather0 = start_gather(swap0, own_second)
    line.mark()
    swap2 = swap(group2, after=(*swap1, gather0[1]))
    skip = own.shape[0]
    own_gathered = [(own, 0), (own_first, 0), (own_second, 0), (gather0[1], 0)]
    gathered0 = end_gather(*gather0, skip)
    gather1 = start_gather(swap1)
    line.mark()
    swap3 = swap(group3, after=(*swap2, gathered0[2][0], gather1[1]))
    gathered1 = end_gather(*gather1)
    gather2 = start_gather(swap2)
    (own_q,) = pack(line, [[(0, c, KEPT) for c in range(3)]], (q_pair,))
    out0 = attend(line, list(queries_of(0, swap2, 2 * part).values()), blocks_of(0, gathered0), outs)
    gathered2 = end_gather(*gather2, after=swap3)
    out1 = attend(line, list(queries_of(1, swap3, 0).values()), blocks_of(1, gathered1), outs)
    back01 = send_back(join(line, [[(x, 0, part), (y, 0, part)] for x, y in zip(out0, out1)]))
    out2 = attend(line, list(queries_of(2, swap3, part).values()), blocks_of(2, gathered2), outs)
    back2 = send_back(out2)
    own01, across01 = core_swap(back01, 2)
    line.mark()
    own2, across2 = core_swap(back2, 1)
    shape = [sds(tokens, width)]
    early = [(0, False), (0, True), (2, False)]
    (attended,) = line.place(functools.partial(place_body, early), shape, own01, across01, own2)
    (attended,) = line.place(
        functools.partial(place_body, [(2, True)]), shape, across2, onto=attended
    )
    return attended


def whole_head_body(q_ref, k_ref, v_ref, out_ref, top, total, accum):
    step = pl.program_id(2)

    @pl.when(step == 0)
    def _():
        top[...] = jnp.full_like(top, -jnp.inf)
        total[...] = jnp.zeros_like(total)
        accum[...] = jnp.zeros_like(accum)

    scores = lax.dot_general(
        q_ref[...], k_ref[...], (((1,), (1,)), ((), ())), preferred_element_type=F32
    )
    new_top = jnp.maximum(top[...], jnp.max(scores, axis=1, keepdims=True))
    weights = jnp.exp2((scores - new_top) * EXPONENT)
    shrink = jnp.exp2((top[...] - new_top) * EXPONENT)
    total[...] = total[...] * shrink + jnp.sum(weights, axis=1, keepdims=True)
    accum[...] = accum[...] * shrink + jnp.dot(
        weights.astype(BF16), v_ref[...], preferred_element_type=F32
    )
    top[...] = new_top

    @pl.when(step == pl.num_programs(2) - 1)
    def _():
        out_ref[...] = (accum[...] / total[...]).astype(BF16)


def normalize(block, gain):
    wide = block.astype(F32)
    mean_sq = jnp.mean(wide * wide, axis=-1, keepdims=True)
    return (wide * lax.rsqrt(mean_sq + 1e-06) * gain).astype(BF16)


def shards_any(queries, keys, values, query_gain, key_gain):
    def regroup(x):
        return lax.all_to_all(x, "head", split_axis=1, concat_axis=0, tiled=True)

    q = regroup(normalize(queries, query_gain))
    k = lax.all_gather(regroup(normalize(keys, key_gain)), "blk", axis=0, tiled=True)
    v = lax.all_gather(regroup(values), "blk", axis=0, tiled=True)
    rows, width = q.shape
    length = k.shape[0]
    q_rows, k_rows = math.gcd(rows, 512), math.gcd(length, 1024)
    result = pl.pallas_call(
        whole_head_body,
        grid=(width // HEAD_DIM, rows // q_rows, length // k_rows),
        out_shape=sds(rows, width),
        in_specs=[
            pl.BlockSpec((q_rows, HEAD_DIM), lambda h, i, j: (i, h)),
            pl.BlockSpec((k_rows, HEAD_DIM), lambda h, i, j: (j, h)),
            pl.BlockSpec((k_rows, HEAD_DIM), lambda h, i, j: (j, h)),
        ],
        out_specs=pl.BlockSpec((q_rows, HEAD_DIM), lambda h, i, j: (i, h)),
        scratch_shapes=[
            pltpu.VMEM((q_rows, 1), F32),
            pltpu.VMEM((q_rows, 1), F32),
            pltpu.VMEM((q_rows, HEAD_DIM), F32),
        ],
        compiler_params=PARAMS,
    )(q, k, v)
    return lax.all_to_all(result, "head", split_axis=0, concat_axis=1, tiled=True)


def solution(mesh):
    fast = mesh.shape["blk"] == 8 and mesh.shape["head"] == 4
    rows = P(AXES, None)
    return jax.shard_map(
        shards_fast if fast else shards_any,
        mesh=mesh,
        in_specs=(rows, rows, rows, P(), P()),
        out_specs=rows,
        check_vma=False,
    )
```

```python
import functools
import math

import jax
import jax.numpy as jnp
from jax import lax
from jax.experimental import pallas as pl
from jax.experimental.pallas import tpu as pltpu
from jax.sharding import PartitionSpec as P

HEAD_DIM = 128
AXES = ("blk", "head")
BF16 = jnp.bfloat16
F32 = jnp.float32
VMEM = pl.BlockSpec(memory_space=pltpu.VMEM)
PARAMS = pltpu.CompilerParams(vmem_limit_bytes=40 * 2**20)
EXPONENT = math.log2(math.e) / math.sqrt(HEAD_DIM)


def nothing_body(out):
    out[...] = jnp.zeros_like(out)


def sds(*shape):
    return jax.ShapeDtypeStruct(shape, BF16)


class Line:
    def __init__(self):
        self.last = ()

    def call(self, body, outs, *args, after=(), flops=0, exps=0):
        behind = (*self.last, *after)
        skip = len(behind)

        def without_last(*refs):
            body(*refs[skip:])

        size = sum(math.prod(a.shape) * a.dtype.itemsize for a in (*args, *outs))
        made = pl.pallas_call(
            without_last,
            out_shape=outs,
            in_specs=[pl.BlockSpec(memory_space=pl.ANY)] * skip
            + [VMEM] * len(args),
            out_specs=[VMEM] * len(outs),
            compiler_params=PARAMS,
            cost_estimate=pl.CostEstimate(flops=flops, bytes_accessed=size, transcendentals=exps),
        )(*behind, *args)
        self.last = made[:1]
        return made

    def place(self, body, outs, *args, onto=None):
        behind = self.last if onto is None else (onto,)
        tokens = outs[0].shape[0]

        def without_last(*refs):
            body(*refs[len(behind) :])

        made = pl.pallas_call(
            without_last,
            out_shape=outs,
            in_specs=[pl.BlockSpec(memory_space=pl.ANY)] * len(behind) + [VMEM] * len(args),
            out_specs=[pl.BlockSpec(memory_space=pl.ANY)],
            scratch_shapes=[
                pltpu.SemaphoreType.DMA((sum(a.shape[0] for a in args) // tokens,))
            ],
            input_output_aliases={} if onto is None else {0: 0},
            compiler_params=PARAMS,
        )(*behind, *args)
        self.last = made[:1]
        return made

    def mark(self):
        self.call(nothing_body, [sds(16, HEAD_DIM)], flops=2 * 10**10)


def read(refs, pieces):
    parts = [refs[source][first : first + rows, :] for source, first, rows in pieces]
    return parts[0] if len(parts) == 1 else jnp.concatenate(parts, axis=0)


def scores_of(q, k):
    return lax.dot_general(q, k, (((1,), (1,)), ((), ())), preferred_element_type=F32)


def absorb(state, scores, v):
    new_top = jnp.max(scores, axis=1, keepdims=True)
    if state is not None:
        top, accum = state
        new_top = jnp.maximum(top, new_top)
    weights = jnp.exp2((scores - new_top) * EXPONENT)
    both = jnp.concatenate([v, jnp.ones_like(v)], axis=1)
    mixed = jnp.dot(weights.astype(BF16), both, preferred_element_type=F32)
    if state is not None:
        mixed = accum * jnp.exp2((top - new_top) * EXPONENT) + mixed
    return new_top, mixed


def attend_body(queries, blocks, count, *refs):
    refs, outs = refs[:count], refs[count:]
    steps = [(pair, block) for pair in range(0, len(queries), 2) for block in blocks]

    def scores_at(step):
        pair, (keys, _) = steps[step]
        return scores_of(read(refs, queries[pair : pair + 2]), read(refs, keys))

    ahead = scores_at(0)
    state = None
    for step, (pair, (keys, values)) in enumerate(steps):
        scores = ahead
        if step + 1 < len(steps):
            ahead = scores_at(step + 1)
        if keys is blocks[0][0]:
            state = None
        state = absorb(state, scores, read(refs, values))
        if keys is not blocks[-1][0]:
            continue
        accum = state[1]
        result = (accum[:, :HEAD_DIM] / accum[:, HEAD_DIM:]).astype(BF16)
        first = pair // 2 * result.shape[0]
        at = 0
        for out in outs:
            low, high = max(at, first), min(at + out.shape[0], first + result.shape[0])
            if low < high:
                out[low - at : high - at, :] = result[low - first : high - first, :]
            at += out.shape[0]


class Arrays:
    def __init__(self):
        self.arrays = []

    def piece(self, array, first, rows):
        for place, known in enumerate(self.arrays):
            if known is array:
                return place, first, rows
        self.arrays.append(array)
        return len(self.arrays) - 1, first, rows

    def pieces(self, parts):
        return [self.piece(*part) for part in parts]


def attend(line, queries, blocks, outs):
    known = Arrays()
    queries = known.pieces(queries)
    blocks = [(known.pieces(keys), known.pieces(values)) for keys, values in blocks]
    pairs = sum(outs) * sum(k[2] for keys, _ in blocks for k in keys)
    return line.call(
        functools.partial(attend_body, queries, blocks, len(known.arrays)),
        [sds(rows, HEAD_DIM) for rows in outs],
        *known.arrays,
        flops=4 * pairs * HEAD_DIM,
        exps=pairs,
    )


KEPT, SECOND, FIRST, OPPOSITE = range(4)
HOPS = (KEPT, SECOND, FIRST, OPPOSITE)


def core_index():
    return lax.rem(lax.axis_index("blk"), 2)


def halves_body(x_ref, other_ref):
    half = x_ref.shape[1] // 2
    other = pl.multiple_of((1 - core_index()) * half, half)
    other_ref[...] = x_ref[:, pl.ds(other, half)]


def normalize_body(x_ref, gain_ref, own_ref, other_ref):
    half = x_ref.shape[1] // 2
    wide = x_ref[...].astype(F32)
    scale = lax.rsqrt(jnp.mean(wide * wide, axis=1, keepdims=True) + 1e-06)
    core = core_index()
    for ref, side in ((own_ref, core), (other_ref, 1 - core)):
        at = pl.ds(pl.multiple_of(side * half, half), half)
        ref[...] = (x_ref[:, at].astype(F32) * scale * gain_ref[:, at]).astype(BF16)


def column(piece, hop):
    z, core = lax.axis_index("head"), core_index()
    low, high = lax.rem(z, 2), lax.div(z, 2)
    if hop in (FIRST, OPPOSITE):
        low, high = lax.rem(low + core, 2), lax.rem(high + 1 - core, 2)
    if hop in (SECOND, OPPOSITE):
        low, high = lax.rem(low + 1 - core, 2), lax.rem(high + core, 2)
    return pl.multiple_of((piece * 4 + high * 2 + low) * HEAD_DIM, HEAD_DIM)


def pack_body(heads, half, *refs):
    ins, outs = refs[: -len(heads)], refs[-len(heads) :]
    for out, group in zip(outs, heads):
        at = 0
        for tensor, piece, hop in group:
            start = column(piece, hop)
            for ref in ins[2 * tensor : 2 * tensor + 2]:
                tokens = ref.shape[0]
                here = start
                if ref.shape[1] != half:
                    here = pl.multiple_of(core_index() * half + start, HEAD_DIM)
                out[at : at + tokens, :] = ref[:, pl.ds(here, HEAD_DIM)]
                at += tokens


def pack(line, heads, tensors, after=()):
    flat = [a for pair in tensors for a in pair]
    tokens = flat[0].shape[0]
    half = min(a.shape[1] for a in flat)
    outs = [sds(2 * tokens * len(group), HEAD_DIM) for group in heads]
    return line.call(functools.partial(pack_body, heads, half), outs, *flat, after=after)


def join_body(layout, count, *refs):
    for out, pieces in zip(refs[count:], layout):
        at = 0
        for source, first, rows in pieces:
            out[at : at + rows, :] = refs[source][first : first + rows, :]
            at += rows


def join(line, layout, after=(), order=()):
    known = Arrays()
    for array in order:
        known.piece(array, 0, 0)
    layout = [known.pieces(parts) for parts in layout]
    outs = [sds(sum(rows for _, _, rows in parts), HEAD_DIM) for parts in layout]
    return line.call(
        functools.partial(join_body, layout, len(known.arrays)), outs, *known.arrays, after=after
    )


def place_body(parts, *refs):
    out, sems = refs[-2:]
    tokens, half = out.shape[0], out.shape[1] // 2
    copies = []
    for ref, (chunk, across) in zip(refs, parts):
        core = 1 - core_index() if across else core_index()
        for place in range(ref.shape[0] // tokens):
            start = core * half + column(chunk + place // 4, place % 4)
            columns = pl.ds(pl.multiple_of(start, HEAD_DIM), HEAD_DIM)
            rows = pl.ds(place * tokens, tokens)
            copies.append(
                pltpu.make_async_copy(ref.at[rows], out.at[:, columns], sems.at[len(copies)])
            )
    for copy in copies:
        copy.start()
    for copy in copies:
        copy.wait()


def permute(array, move):
    pairs = []
    for y in range(2):
        for x in range(2):
            for core in range(2):
                for z in range(4):
                    to = move(y, x, core, z)
                    pairs.append(
                        ((y * 4 + x * 2 + core) * 4 + z, (to[0] * 4 + to[1] * 2 + to[2]) * 4 + to[3])
                    )
    return lax.ppermute(array, AXES, pairs)


def other_core(array):
    return permute(array, lambda y, x, core, z: (y, x, 1 - core, z))


def hop_z(array, hop):
    def move(y, x, core, z):
        first, second = (2, 1) if core == 0 else (1, 2)
        return y, x, core, z ^ {FIRST: first, SECOND: second, OPPOSITE: 3}[hop]

    return permute(array, move)


def hop_xy(array, hop):
    def move(y, x, core, z):
        return (y, 1 - x, core, z) if (hop == FIRST) == (core == 0) else (1 - y, x, core, z)

    return permute(array, move)


def shards_fast(queries, keys, values, query_gain, key_gain):
    tokens, width = queries.shape
    half, part = width // 2, 2 * tokens
    rest = 3 * part
    query_gain, key_gain = query_gain.reshape(1, width), key_gain.reshape(1, width)
    line = Line()

    def swap_halves(x, gain):
        own, other = line.call(normalize_body, [sds(tokens, half)] * 2, x, gain)
        return own, other_core(other)

    k_pair = swap_halves(keys, key_gain)
    (v_other,) = line.call(halves_body, [sds(tokens, half)], values)
    v_pair = (values, other_core(v_other))
    q_pair = swap_halves(queries, query_gain)
    tensors = (k_pair, v_pair, q_pair)
    k, v, q = range(3)

    def swap(heads, after=()):
        used = sorted({t for t, _ in heads})
        groups = [[(used.index(t), c, hop) for t, c in heads] for hop in HOPS[1:]]
        outs = pack(line, groups, [tensors[t] for t in used], after)
        return [hop_z(out, hop) for hop, out in zip(HOPS[1:], outs)]

    def slots(swapped, first, rows):
        return [(array, first, rows) for array in swapped]

    def start_gather(swapped, *ahead):
        layout = slots(swapped, 0, part) + slots(swapped, part, part)
        (block,) = join(line, [[(a, 0, a.shape[0]) for a in ahead] + layout])
        return block, hop_xy(block, FIRST)

    def end_gather(block, got, skip=0, after=()):
        rows = block.shape[0] - skip
        (both,) = join(line, [[(block, skip, rows), (got, skip, rows)]], after)
        more = hop_xy(both, SECOND)
        return [(block, skip), (got, skip), (more, 0), (more, rows)]

    def blocks_of(chunk, gathered):
        blocks = []
        for (kept, kept_at), (array, at) in zip(own_gathered, gathered):
            keys = [(kept, kept_at + 2 * chunk * part, part), (array, at, rest)]
            blocks.append((keys, [(a, first + rows, rows) for a, first, rows in keys]))
        return [
            (low[0] + high[0], low[1] + high[1]) for low, high in zip(blocks[::2], blocks[1::2])
        ]

    def queries_of(chunk, swapped, first):
        return dict(zip(HOPS, [(own_q, chunk * part, part)] + slots(swapped, first, part)))

    def core_swap(back, chunks):
        kept, second, first, opposite = back
        own, other = [], []
        for c in range(chunks):
            own += [(a, 2 * c * tokens, tokens) for a in back]
            other += [(a, (2 * c + 1) * tokens, tokens) for a in (kept, first, second, opposite)]
        own, across = join(line, [own, other], order=(opposite, first, second, kept) if chunks == 1 else ())
        return own, other_core(across)

    def send_back(outs):
        return [outs[KEPT]] + [hop_z(outs[hop], hop) for hop in HOPS[1:]]

    group0, group1 = [(k, 0), (v, 0)], [(k, 1), (v, 1)]
    group2, group3 = [(k, 2), (v, 2), (q, 0)], [(q, 1), (q, 2)]
    outs = [part] * 4

    swap0 = swap(group0)
    (own,) = pack(line, [[(t, c, KEPT) for c in range(3) for t in (k, v)]], tensors[:2])
    own_first, own_second = hop_xy(own, FIRST), hop_xy(own, SECOND)
    line.mark()
    swap1 = swap(group1, after=(*swap0, own_first, own_second))
    gather0 = start_gather(swap0, own_second)
    line.mark()
    swap2 = swap(group2, after=(*swap1, gather0[1]))
    skip = own.shape[0]
    own_gathered = [(own, 0), (own_first, 0), (own_second, 0), (gather0[1], 0)]
    gathered0 = end_gather(*gather0, skip)
    gather1 = start_gather(swap1)
    line.mark()
    swap3 = swap(group3, after=(*swap2, gathered0[2][0], gather1[1]))
    gathered1 = end_gather(*gather1)
    gather2 = start_gather(swap2)
    (own_q,) = pack(line, [[(0, c, KEPT) for c in range(3)]], (q_pair,))
    out0 = attend(line, list(queries_of(0, swap2, 2 * part).values()), blocks_of(0, gathered0), outs)
    gathered2 = end_gather(*gather2, after=swap3)
    slots1, blocks1 = queries_of(1, swap3, 0), blocks_of(1, gathered1)

    def both(hops):
        late = attend(line, [slots1[hop] for hop in hops], blocks1, [part] * 2)
        return join(line, [[(out0[hop], 0, part), (x, 0, part)] for hop, x in zip(hops, late)])

    opposite, kept = both((OPPOSITE, KEPT))
    opposite = hop_z(opposite, OPPOSITE)
    second, first = both((SECOND, FIRST))
    back01 = [kept, hop_z(second, SECOND), hop_z(first, FIRST), opposite]
    out2 = attend(line, list(queries_of(2, swap3, part).values()), blocks_of(2, gathered2), outs)
    back2 = send_back(out2)
    own01, across01 = core_swap(back01, 2)
    line.mark()
    own2, across2 = core_swap(back2, 1)
    shape = [sds(tokens, width)]
    early = [(0, False), (0, True), (2, False)]
    (attended,) = line.place(functools.partial(place_body, early), shape, own01, across01, own2)
    (attended,) = line.place(
        functools.partial(place_body, [(2, True)]), shape, across2, onto=attended
    )
    return attended


def whole_head_body(q_ref, k_ref, v_ref, out_ref, top, total, accum):
    step = pl.program_id(2)

    @pl.when(step == 0)
    def _():
        top[...] = jnp.full_like(top, -jnp.inf)
        total[...] = jnp.zeros_like(total)
        accum[...] = jnp.zeros_like(accum)

    scores = lax.dot_general(
        q_ref[...], k_ref[...], (((1,), (1,)), ((), ())), preferred_element_type=F32
    )
    new_top = jnp.maximum(top[...], jnp.max(scores, axis=1, keepdims=True))
    weights = jnp.exp2((scores - new_top) * EXPONENT)
    shrink = jnp.exp2((top[...] - new_top) * EXPONENT)
    total[...] = total[...] * shrink + jnp.sum(weights, axis=1, keepdims=True)
    accum[...] = accum[...] * shrink + jnp.dot(
        weights.astype(BF16), v_ref[...], preferred_element_type=F32
    )
    top[...] = new_top

    @pl.when(step == pl.num_programs(2) - 1)
    def _():
        out_ref[...] = (accum[...] / total[...]).astype(BF16)


def normalize(block, gain):
    wide = block.astype(F32)
    mean_sq = jnp.mean(wide * wide, axis=-1, keepdims=True)
    return (wide * lax.rsqrt(mean_sq + 1e-06) * gain).astype(BF16)


def shards_any(queries, keys, values, query_gain, key_gain):
    def regroup(x):
        return lax.all_to_all(x, "head", split_axis=1, concat_axis=0, tiled=True)

    q = regroup(normalize(queries, query_gain))
    k = lax.all_gather(regroup(normalize(keys, key_gain)), "blk", axis=0, tiled=True)
    v = lax.all_gather(regroup(values), "blk", axis=0, tiled=True)
    rows, width = q.shape
    length = k.shape[0]
    q_rows, k_rows = math.gcd(rows, 512), math.gcd(length, 1024)
    result = pl.pallas_call(
        whole_head_body,
        grid=(width // HEAD_DIM, rows // q_rows, length // k_rows),
        out_shape=sds(rows, width),
        in_specs=[
            pl.BlockSpec((q_rows, HEAD_DIM), lambda h, i, j: (i, h)),
            pl.BlockSpec((k_rows, HEAD_DIM), lambda h, i, j: (j, h)),
            pl.BlockSpec((k_rows, HEAD_DIM), lambda h, i, j: (j, h)),
        ],
        out_specs=pl.BlockSpec((q_rows, HEAD_DIM), lambda h, i, j: (i, h)),
        scratch_shapes=[
            pltpu.VMEM((q_rows, 1), F32),
            pltpu.VMEM((q_rows, 1), F32),
            pltpu.VMEM((q_rows, HEAD_DIM), F32),
        ],
        compiler_params=PARAMS,
    )(q, k, v)
    return lax.all_to_all(result, "head", split_axis=0, concat_axis=1, tiled=True)


def solution(mesh):
    fast = mesh.shape["blk"] == 8 and mesh.shape["head"] == 4
    rows = P(AXES, None)
    return jax.shard_map(
        shards_fast if fast else shards_any,
        mesh=mesh,
        in_specs=(rows, rows, rows, P(), P()),
        out_specs=rows,
        check_vma=False,
    )
```

```python
import functools
import math

import jax
import jax.numpy as jnp
from jax import lax
from jax.experimental import pallas as pl
from jax.experimental.pallas import tpu as pltpu
from jax.sharding import PartitionSpec as P

HEAD_DIM = 128
AXES = ("blk", "head")
BF16 = jnp.bfloat16
F32 = jnp.float32
VMEM = pl.BlockSpec(memory_space=pltpu.VMEM)
PARAMS = pltpu.CompilerParams(vmem_limit_bytes=40 * 2**20)
EXPONENT = math.log2(math.e) / math.sqrt(HEAD_DIM)


def nothing_body(out):
    out[...] = jnp.zeros_like(out)


def sds(*shape):
    return jax.ShapeDtypeStruct(shape, BF16)


class Line:
    def __init__(self):
        self.last = ()

    def call(self, body, outs, *args, after=(), flops=0, exps=0):
        behind = (*self.last, *after)
        skip = len(behind)

        def without_last(*refs):
            body(*refs[skip:])

        size = sum(math.prod(a.shape) * a.dtype.itemsize for a in (*args, *outs))
        made = pl.pallas_call(
            without_last,
            out_shape=outs,
            in_specs=[pl.BlockSpec(memory_space=pl.ANY)] * skip
            + [VMEM] * len(args),
            out_specs=[VMEM] * len(outs),
            compiler_params=PARAMS,
            cost_estimate=pl.CostEstimate(flops=flops, bytes_accessed=size, transcendentals=exps),
        )(*behind, *args)
        self.last = made[:1]
        return made

    def place(self, body, outs, *args, onto=None):
        behind = self.last if onto is None else (onto,)
        tokens = outs[0].shape[0]

        def without_last(*refs):
            body(*refs[len(behind) :])

        made = pl.pallas_call(
            without_last,
            out_shape=outs,
            in_specs=[pl.BlockSpec(memory_space=pl.ANY)] * len(behind) + [VMEM] * len(args),
            out_specs=[pl.BlockSpec(memory_space=pl.ANY)],
            scratch_shapes=[
                pltpu.SemaphoreType.DMA((sum(a.shape[0] for a in args) // tokens,))
            ],
            input_output_aliases={} if onto is None else {0: 0},
            compiler_params=PARAMS,
        )(*behind, *args)
        self.last = made[:1]
        return made

    def mark(self):
        self.call(nothing_body, [sds(16, HEAD_DIM)], flops=2 * 10**10)


def read(refs, pieces):
    parts = [refs[source][first : first + rows, :] for source, first, rows in pieces]
    return parts[0] if len(parts) == 1 else jnp.concatenate(parts, axis=0)


def scores_of(q, k):
    return lax.dot_general(q, k, (((1,), (1,)), ((), ())), preferred_element_type=F32)


def absorb(state, scores, v):
    new_top = jnp.max(scores, axis=1, keepdims=True)
    if state is not None:
        top, accum = state
        new_top = jnp.maximum(top, new_top)
    weights = jnp.exp2((scores - new_top) * EXPONENT)
    both = jnp.concatenate([v, jnp.ones_like(v)], axis=1)
    mixed = jnp.dot(weights.astype(BF16), both, preferred_element_type=F32)
    if state is not None:
        mixed = accum * jnp.exp2((top - new_top) * EXPONENT) + mixed
    return new_top, mixed


def attend_body(queries, blocks, count, *refs):
    refs, outs = refs[:count], refs[count:]
    steps = [(pair, block) for pair in range(0, len(queries), 2) for block in blocks]

    def scores_at(step):
        pair, (keys, _) = steps[step]
        return scores_of(read(refs, queries[pair : pair + 2]), read(refs, keys))

    ahead = scores_at(0)
    state = None
    for step, (pair, (keys, values)) in enumerate(steps):
        scores = ahead
        if step + 1 < len(steps):
            ahead = scores_at(step + 1)
        if keys is blocks[0][0]:
            state = None
        state = absorb(state, scores, read(refs, values))
        if keys is not blocks[-1][0]:
            continue
        accum = state[1]
        result = (accum[:, :HEAD_DIM] / accum[:, HEAD_DIM:]).astype(BF16)
        first = pair // 2 * result.shape[0]
        at = 0
        for out in outs:
            low, high = max(at, first), min(at + out.shape[0], first + result.shape[0])
            if low < high:
                out[low - at : high - at, :] = result[low - first : high - first, :]
            at += out.shape[0]


class Arrays:
    def __init__(self):
        self.arrays = []

    def piece(self, array, first, rows):
        for place, known in enumerate(self.arrays):
            if known is array:
                return place, first, rows
        self.arrays.append(array)
        return len(self.arrays) - 1, first, rows

    def pieces(self, parts):
        return [self.piece(*part) for part in parts]


def attend(line, queries, blocks, outs):
    known = Arrays()
    queries = known.pieces(queries)
    blocks = [(known.pieces(keys), known.pieces(values)) for keys, values in blocks]
    pairs = sum(outs) * sum(k[2] for keys, _ in blocks for k in keys)
    return line.call(
        functools.partial(attend_body, queries, blocks, len(known.arrays)),
        [sds(rows, HEAD_DIM) for rows in outs],
        *known.arrays,
        flops=4 * pairs * HEAD_DIM,
        exps=pairs,
    )


KEPT, SECOND, FIRST, OPPOSITE = range(4)
HOPS = (KEPT, SECOND, FIRST, OPPOSITE)


def core_index():
    return lax.rem(lax.axis_index("blk"), 2)


def halves_body(x_ref, other_ref):
    half = x_ref.shape[1] // 2
    other = pl.multiple_of((1 - core_index()) * half, half)
    other_ref[...] = x_ref[:, pl.ds(other, half)]


def normalize_body(x_ref, gain_ref, own_ref, other_ref):
    half = x_ref.shape[1] // 2
    wide = x_ref[...].astype(F32)
    scale = lax.rsqrt(jnp.mean(wide * wide, axis=1, keepdims=True) + 1e-06)
    core = core_index()
    for ref, side in ((own_ref, core), (other_ref, 1 - core)):
        at = pl.ds(pl.multiple_of(side * half, half), half)
        ref[...] = (x_ref[:, at].astype(F32) * scale * gain_ref[:, at]).astype(BF16)


def column(piece, hop):
    z, core = lax.axis_index("head"), core_index()
    low, high = lax.rem(z, 2), lax.div(z, 2)
    if hop in (FIRST, OPPOSITE):
        low, high = lax.rem(low + core, 2), lax.rem(high + 1 - core, 2)
    if hop in (SECOND, OPPOSITE):
        low, high = lax.rem(low + 1 - core, 2), lax.rem(high + core, 2)
    return pl.multiple_of((piece * 4 + high * 2 + low) * HEAD_DIM, HEAD_DIM)


def pack_body(heads, half, *refs):
    ins, outs = refs[: -len(heads)], refs[-len(heads) :]
    for out, group in zip(outs, heads):
        at = 0
        for tensor, piece, hop in group:
            start = column(piece, hop)
            for ref in ins[2 * tensor : 2 * tensor + 2]:
                tokens = ref.shape[0]
                here = start
                if ref.shape[1] != half:
                    here = pl.multiple_of(core_index() * half + start, HEAD_DIM)
                out[at : at + tokens, :] = ref[:, pl.ds(here, HEAD_DIM)]
                at += tokens


def pack(line, heads, tensors, after=()):
    flat = [a for pair in tensors for a in pair]
    tokens = flat[0].shape[0]
    half = min(a.shape[1] for a in flat)
    outs = [sds(2 * tokens * len(group), HEAD_DIM) for group in heads]
    return line.call(functools.partial(pack_body, heads, half), outs, *flat, after=after)


def join_body(layout, count, *refs):
    for out, pieces in zip(refs[count:], layout):
        at = 0
        for source, first, rows in pieces:
            out[at : at + rows, :] = refs[source][first : first + rows, :]
            at += rows


def join(line, layout, after=(), order=()):
    known = Arrays()
    for array in order:
        known.piece(array, 0, 0)
    layout = [known.pieces(parts) for parts in layout]
    outs = [sds(sum(rows for _, _, rows in parts), HEAD_DIM) for parts in layout]
    return line.call(
        functools.partial(join_body, layout, len(known.arrays)), outs, *known.arrays, after=after
    )


def place_body(parts, *refs):
    out, sems = refs[-2:]
    tokens, half = out.shape[0], out.shape[1] // 2
    copies = []
    for ref, (chunk, across) in zip(refs, parts):
        core = 1 - core_index() if across else core_index()
        for place in range(ref.shape[0] // tokens):
            start = core * half + column(chunk + place // 4, place % 4)
            columns = pl.ds(pl.multiple_of(start, HEAD_DIM), HEAD_DIM)
            rows = pl.ds(place * tokens, tokens)
            copies.append(
                pltpu.make_async_copy(ref.at[rows], out.at[:, columns], sems.at[len(copies)])
            )
    for copy in copies:
        copy.start()
    for copy in copies:
        copy.wait()


def permute(array, move):
    pairs = []
    for y in range(2):
        for x in range(2):
            for core in range(2):
                for z in range(4):
                    to = move(y, x, core, z)
                    pairs.append(
                        ((y * 4 + x * 2 + core) * 4 + z, (to[0] * 4 + to[1] * 2 + to[2]) * 4 + to[3])
                    )
    return lax.ppermute(array, AXES, pairs)


def other_core(array):
    return permute(array, lambda y, x, core, z: (y, x, 1 - core, z))


def hop_z(array, hop):
    def move(y, x, core, z):
        first, second = (2, 1) if core == 0 else (1, 2)
        return y, x, core, z ^ {FIRST: first, SECOND: second, OPPOSITE: 3}[hop]

    return permute(array, move)


def hop_xy(array, hop):
    def move(y, x, core, z):
        return (y, 1 - x, core, z) if (hop == FIRST) == (core == 0) else (1 - y, x, core, z)

    return permute(array, move)


def shards_fast(queries, keys, values, query_gain, key_gain):
    tokens, width = queries.shape
    half, part = width // 2, 2 * tokens
    rest = 3 * part
    query_gain, key_gain = query_gain.reshape(1, width), key_gain.reshape(1, width)
    line = Line()

    def swap_halves(x, gain):
        own, other = line.call(normalize_body, [sds(tokens, half)] * 2, x, gain)
        return own, other_core(other)

    k_pair = swap_halves(keys, key_gain)
    (v_other,) = line.call(halves_body, [sds(tokens, half)], values)
    v_pair = (values, other_core(v_other))
    q_pair = swap_halves(queries, query_gain)
    tensors = (k_pair, v_pair, q_pair)
    k, v, q = range(3)

    def swap(heads, after=()):
        used = sorted({t for t, _ in heads})
        groups = [[(used.index(t), c, hop) for t, c in heads] for hop in HOPS[1:]]
        outs = pack(line, groups, [tensors[t] for t in used], after)
        return [hop_z(out, hop) for hop, out in zip(HOPS[1:], outs)]

    def slots(swapped, first, rows):
        return [(array, first, rows) for array in swapped]

    def start_gather(swapped, *ahead):
        layout = slots(swapped, 0, part) + slots(swapped, part, part)
        (block,) = join(line, [[(a, 0, a.shape[0]) for a in ahead] + layout])
        return block, hop_xy(block, FIRST)

    def end_gather(block, got, skip=0, after=()):
        rows = block.shape[0] - skip
        (both,) = join(line, [[(block, skip, rows), (got, skip, rows)]], after)
        more = hop_xy(both, SECOND)
        return [(block, skip), (got, skip), (more, 0), (more, rows)]

    def blocks_of(chunk, gathered):
        blocks = []
        for (kept, kept_at), (array, at) in zip(own_gathered, gathered):
            keys = [(kept, kept_at + 2 * chunk * part, part), (array, at, rest)]
            blocks.append((keys, [(a, first + rows, rows) for a, first, rows in keys]))
        return [
            (low[0] + high[0], low[1] + high[1]) for low, high in zip(blocks[::2], blocks[1::2])
        ]

    def queries_of(chunk, swapped, first):
        return dict(zip(HOPS, [(own_q, chunk * part, part)] + slots(swapped, first, part)))

    def core_swap(back, chunks):
        kept, second, first, opposite = back
        own, other = [], []
        for c in range(chunks):
            own += [(a, 2 * c * tokens, tokens) for a in back]
            other += [(a, (2 * c + 1) * tokens, tokens) for a in (kept, first, second, opposite)]
        own, across = join(line, [own, other], order=(opposite, first, second, kept) if chunks == 1 else ())
        return own, other_core(across)

    def send_back(outs):
        return [outs[KEPT]] + [hop_z(outs[hop], hop) for hop in HOPS[1:]]

    group0, group1 = [(k, 0), (v, 0)], [(k, 1), (v, 1)]
    group2, group3 = [(k, 2), (v, 2), (q, 0)], [(q, 1), (q, 2)]
    outs = [part] * 4

    swap0 = swap(group0)
    (own,) = pack(line, [[(t, c, KEPT) for c in range(3) for t in (k, v)]], tensors[:2])
    own_first, own_second = hop_xy(own, FIRST), hop_xy(own, SECOND)
    line.mark()
    swap1 = swap(group1, after=(*swap0, own_first, own_second))
    gather0 = start_gather(swap0, own_second)
    line.mark()
    swap2 = swap(group2, after=(*swap1, gather0[1]))
    skip = own.shape[0]
    own_gathered = [(own, 0), (own_first, 0), (own_second, 0), (gather0[1], 0)]
    gathered0 = end_gather(*gather0, skip)
    gather1 = start_gather(swap1)
    line.mark()
    swap3 = swap(group3, after=(*swap2, gathered0[2][0], gather1[1]))
    gathered1 = end_gather(*gather1)
    gather2 = start_gather(swap2)
    (own_q,) = pack(line, [[(0, c, KEPT) for c in range(3)]], (q_pair,))
    out0 = attend(line, list(queries_of(0, swap2, 2 * part).values()), blocks_of(0, gathered0), outs)
    gathered2 = end_gather(*gather2, after=swap3)
    slots1, blocks1 = queries_of(1, swap3, 0), blocks_of(1, gathered1)

    def both(hops):
        late = attend(line, [slots1[hop] for hop in hops], blocks1, [part] * 2)
        return join(line, [[(out0[hop], 0, part), (x, 0, part)] for hop, x in zip(hops, late)])

    opposite, kept = both((OPPOSITE, KEPT))
    opposite = hop_z(opposite, OPPOSITE)
    second, first = both((SECOND, FIRST))
    back01 = [kept, hop_z(second, SECOND), hop_z(first, FIRST), opposite]
    slots2, blocks2 = queries_of(2, swap3, part), blocks_of(2, gathered2)
    opposite2, kept2 = attend(line, [slots2[OPPOSITE], slots2[KEPT]], blocks2, [part] * 2)
    opposite2 = hop_z(opposite2, OPPOSITE)
    second2, first2 = attend(line, [slots2[SECOND], slots2[FIRST]], blocks2, [part] * 2)
    back2 = [kept2, hop_z(second2, SECOND), hop_z(first2, FIRST), opposite2]
    own01, across01 = core_swap(back01, 2)
    line.mark()
    own2, across2 = core_swap(back2, 1)
    shape = [sds(tokens, width)]
    early = [(0, False), (0, True), (2, False)]
    (attended,) = line.place(functools.partial(place_body, early), shape, own01, across01, own2)
    (attended,) = line.place(
        functools.partial(place_body, [(2, True)]), shape, across2, onto=attended
    )
    return attended


def whole_head_body(q_ref, k_ref, v_ref, out_ref, top, total, accum):
    step = pl.program_id(2)

    @pl.when(step == 0)
    def _():
        top[...] = jnp.full_like(top, -jnp.inf)
        total[...] = jnp.zeros_like(total)
        accum[...] = jnp.zeros_like(accum)

    scores = lax.dot_general(
        q_ref[...], k_ref[...], (((1,), (1,)), ((), ())), preferred_element_type=F32
    )
    new_top = jnp.maximum(top[...], jnp.max(scores, axis=1, keepdims=True))
    weights = jnp.exp2((scores - new_top) * EXPONENT)
    shrink = jnp.exp2((top[...] - new_top) * EXPONENT)
    total[...] = total[...] * shrink + jnp.sum(weights, axis=1, keepdims=True)
    accum[...] = accum[...] * shrink + jnp.dot(
        weights.astype(BF16), v_ref[...], preferred_element_type=F32
    )
    top[...] = new_top

    @pl.when(step == pl.num_programs(2) - 1)
    def _():
        out_ref[...] = (accum[...] / total[...]).astype(BF16)


def normalize(block, gain):
    wide = block.astype(F32)
    mean_sq = jnp.mean(wide * wide, axis=-1, keepdims=True)
    return (wide * lax.rsqrt(mean_sq + 1e-06) * gain).astype(BF16)


def shards_any(queries, keys, values, query_gain, key_gain):
    def regroup(x):
        return lax.all_to_all(x, "head", split_axis=1, concat_axis=0, tiled=True)

    q = regroup(normalize(queries, query_gain))
    k = lax.all_gather(regroup(normalize(keys, key_gain)), "blk", axis=0, tiled=True)
    v = lax.all_gather(regroup(values), "blk", axis=0, tiled=True)
    rows, width = q.shape
    length = k.shape[0]
    q_rows, k_rows = math.gcd(rows, 512), math.gcd(length, 1024)
    result = pl.pallas_call(
        whole_head_body,
        grid=(width // HEAD_DIM, rows // q_rows, length // k_rows),
        out_shape=sds(rows, width),
        in_specs=[
            pl.BlockSpec((q_rows, HEAD_DIM), lambda h, i, j: (i, h)),
            pl.BlockSpec((k_rows, HEAD_DIM), lambda h, i, j: (j, h)),
            pl.BlockSpec((k_rows, HEAD_DIM), lambda h, i, j: (j, h)),
        ],
        out_specs=pl.BlockSpec((q_rows, HEAD_DIM), lambda h, i, j: (i, h)),
        scratch_shapes=[
            pltpu.VMEM((q_rows, 1), F32),
            pltpu.VMEM((q_rows, 1), F32),
            pltpu.VMEM((q_rows, HEAD_DIM), F32),
        ],
        compiler_params=PARAMS,
    )(q, k, v)
    return lax.all_to_all(result, "head", split_axis=0, concat_axis=1, tiled=True)


def solution(mesh):
    fast = mesh.shape["blk"] == 8 and mesh.shape["head"] == 4
    rows = P(AXES, None)
    return jax.shard_map(
        shards_fast if fast else shards_any,
        mesh=mesh,
        in_specs=(rows, rows, rows, P(), P()),
        out_specs=rows,
        check_vma=False,
    )
```
